32 devices in a mesh: query: 4 (over y, x), corpus: 8 (over z, core).
Axes of the slice: x: 2, y: 2, z: 4, core: 2. Of those that a mesh axis runs over, the one named last changes fastest.
Arguments:
- queries: float32 [32, 32, 128], P(('query', 'corpus')), may hold values from -6 to 6
- passages: float32 [128, 180, 128], P(('query', 'corpus')), may hold values from -0.5 to 0.5
- clusters: int32 [128, 180], P(('query', 'corpus')), may hold values from 0 to 23
- lengths: int32 [128], P(('query', 'corpus')), may hold values from 45 to 180, as said below
- feedback: int32 [32, 3], replicated, may hold values from 0 to 127, as said below
- ranks: int32 [32, 24], replicated, may hold values from 0 to 23, each once within a row
- cand_local: int32 [32, 64], P(None, ('query', 'corpus')), may hold values from 0 to 3
- cand_count: int32 [32, 32], P(None, ('query', 'corpus')), may hold values from 1 to 2, as said below
Outputs:
- scores: float32 [32, 64], P(('query', 'corpus'))
The draws below stay inside these ranges and needn't reach their ends.
Inputs may be any that keep to these rules, and one draw needn't show every extreme that they name: `lengths`: some passages fill all 180 slots of their tile. `cand_count`: each query fills all 2 slots on at least one device. The passages of exactly 3 of the (query, feedback) pairs lie on each device. `ranks`: each row is a permutation of 0 to 23.
All inputs are finite; a program needn't handle non-finite values.
Results may differ from the reference program's by a relative error of at most 0.0003.
Values sent between devices are 32-bit elements; how exact they have to be, the bound alone decides.
No kernel may reach another device: no remote copies, remote signals or barrier semaphores. Data moves between devices by JAX's collectives and lax.ppermute only.
A program may use at most 64 MiB of HBM per device.

```python
import jax
import jax.numpy as jnp
from jax import lax

DIM = 128
QL = 32
PL = 180
FB = 3
NCENT = 24
EXP = 10
CAP = 2
Q_DEV = 1
P_DEV = 4
QUERIES = 32
PASSAGES = 128
SLOTS = 64
DEVICES = 32


def draw_lengths(key, part):
    first, second = jax.random.split(key)
    common = jax.random.randint(first, (PASSAGES,), PL // 4, PL + 1)
    offset = jax.random.randint(second, (), 0, 16)
    filled = jnp.arange(PASSAGES) % 16 == offset
    return jnp.where(filled, PL, common).astype(jnp.int32)


def draw_cand_count(key, part):
    first, second = jax.random.split(key)
    common = jax.random.randint(first, (QUERIES, DEVICES), 1, CAP + 1)
    chosen = jax.random.randint(second, (QUERIES, 1), 0, DEVICES)
    filled = jnp.arange(DEVICES)[None, :] == chosen
    return jnp.where(filled, CAP, common).astype(jnp.int32)


def draw_feedback(key, part):
    first, second = jax.random.split(jax.random.fold_in(key, 7))
    pairs = QUERIES * FB
    order = jax.random.permutation(first, pairs)
    device_of = order // (Q_DEV * FB)
    local = jax.random.randint(second, (pairs,), 0, P_DEV)
    return (device_of * P_DEV + local).reshape(QUERIES, FB).astype(jnp.int32)


def touch_ends(array, rng, least, high):
    dims = array.shape
    index_at = [jax.random.randint(jax.random.fold_in(rng, axis), (), 0, dims[axis]) for axis in range(len(dims))]
    array = array.at[tuple(index_at)].set(least)
    longest = dims.index(max(dims))
    index_at[longest] = (index_at[longest] + 1) % dims[longest]
    return array.at[tuple(index_at)].set(high)


def levels(key, extent, cuts, low, largest):
    gain, own = 1.0, jax.random.fold_in(key, 6)
    for dim, parts in cuts:
        steps = jnp.exp(jax.random.uniform(jax.random.fold_in(own, dim), (parts,), jnp.float32, low / len(cuts), largest / len(cuts)))
        gain = gain * jnp.repeat(steps, extent[dim] // parts).reshape([-1 if axis == dim else 1 for axis in range(len(extent))])
    return gain


def centred(stream_key, shape, width, most, shards=(), held_as=jnp.bfloat16):
    values = jax.random.normal(stream_key, shape, jnp.float32) * width
    if len(shards) > 0:
        values = levels(stream_key, shape, shards, -0.22, 0.18) * values
    return jnp.clip(values, min=-most, max=most).astype(held_as)


def setup_inputs(seed: int = 0) -> dict:
    key_of = jax.random.split(jax.random.key(seed), 9)
    return {
        "queries": centred(key_of[0], (QUERIES, QL, DIM), 1.0, 6.0, ((0, 32),), jnp.float32),
        "passages": centred(key_of[1], (PASSAGES, PL, DIM), DIM ** -0.5, 0.5, ((0, 32),), jnp.float32),
        "clusters": touch_ends(jax.random.randint(key_of[2], (PASSAGES, PL), 0, NCENT), jax.random.fold_in(key_of[2], 1), 0, NCENT - 1).astype(jnp.int32),
        "lengths": draw_lengths(jax.random.fold_in(key_of[8], 71), 0),
        "feedback": draw_feedback(jax.random.fold_in(key_of[8], 71), 0),
        "ranks": jax.vmap(lambda own: jax.random.permutation(own, NCENT))(jax.random.split(key_of[5], QUERIES)).reshape((QUERIES, NCENT)).astype(jnp.int32),
        "cand_local": touch_ends(jax.random.randint(key_of[6], (QUERIES, SLOTS), 0, P_DEV), jax.random.fold_in(key_of[6], 1), 0, P_DEV - 1).astype(jnp.int32),
        "cand_count": draw_cand_count(jax.random.fold_in(key_of[8], 71), 0),
    }


beta_prf = 0.5
highest = lax.Precision.HIGHEST

def idf_weights():
    order = jnp.arange(EXP).astype(jnp.float32)
    return beta_prf * jnp.log((NCENT + 1.0) / (order + 1.0))

def expand_tokens(tokens, sums, ranking):
    scale = lax.rsqrt(lax.optimization_barrier(jnp.mean(sums * sums, axis=-1, keepdims=True)) + 1e-05)
    centroid = sums * scale
    select = (ranking[:, None, :] == jnp.arange(EXP, dtype=jnp.int32)[None, :, None]).astype(jnp.float32)
    extra = jnp.einsum('njk,nkd->njd', select, centroid, precision=highest)
    extra = extra * idf_weights()[None, :, None]
    return jnp.concatenate([tokens, extra], axis=1)

def maxsim(expanded, tiles, alive):
    similar = jnp.einsum('ed,spd->sep', expanded, tiles, precision=highest)
    similar = jnp.where(alive[:, None, :], similar, -1e+30)
    return lax.optimization_barrier(jnp.sum(lax.optimization_barrier(jnp.max(similar, axis=2)), axis=1)) / QL

def reference(queries, passages, clusters, lengths, feedback, ranks, cand_local, cand_count):
    token_axis = jnp.arange(PL, dtype=jnp.int32)
    centre_axis = jnp.arange(NCENT, dtype=jnp.int32)

    def feedback_sums(feed_row):
        tiles = passages[feed_row]
        alive = token_axis[None, :] < lengths[feed_row][:, None]
        member = ((clusters[feed_row][:, None, :] == centre_axis[None, :, None]) & alive[:, None, :]).astype(jnp.float32)
        return jnp.einsum('fkt,ftd->kd', member, tiles, precision=highest)
    sums = lax.map(feedback_sums, feedback)
    expanded = expand_tokens(queries, sums, ranks)
    slot_axis = jnp.arange(SLOTS, dtype=jnp.int32)
    owner = slot_axis // CAP

    def score_query(items):
        row_expanded, row_local, row_count = items
        global_ids = (owner * P_DEV + row_local).astype(jnp.int32)
        tiles = passages[global_ids]
        alive = token_axis[None, :] < lengths[global_ids][:, None]
        values = maxsim(row_expanded, tiles, alive)
        valid = slot_axis % CAP < row_count[owner]
        return jnp.where(valid, values, jnp.zeros_like(values))
    return lax.map(score_query, (expanded, cand_local, cand_count))
```

```python
import functools

import jax
import jax.numpy as jnp
from jax import lax
from jax.experimental import pallas as pl
from jax.experimental.pallas import tpu as pltpu
from jax.sharding import PartitionSpec as P

DIM = 128
QL = 32
NCENT = 24
EXP = 10
CAP = 2
FB = 3
BETA = 0.5
AXES = ("query", "corpus")
ID_ROW = 31
CAND_ROW = 32
HIGHEST = lax.Precision.HIGHEST


def iota(shape, axis):
    return lax.broadcasted_iota(jnp.int32, shape, axis)


def spread(index, masks):
    total = 0
    for k, mask in enumerate(masks):
        total = total | (((index >> k) & 1) * mask)
    return total


def gather_bits(device, masks):
    total = 0
    for k, mask in enumerate(masks):
        total = total | (jnp.where((device & mask) != 0, 1, 0) << k)
    return total


def pairs_kernel(queries_n, held, tokens, pos_ref, len_ref, tiles_ref, clusters_ref, feedback_ref, ranks_ref,
                 local_ref, count_ref, masked_ref, pay_ref):
    pos = pos_ref[0]
    per_tile = 8 // held
    row = iota((8, DIM), 0)
    limit = jnp.zeros((8, DIM), jnp.int32)
    for p in range(held):
        limit = jnp.where(row % held == p, len_ref[p], limit)
    first = tiles_ref[0:held, :]
    first = jnp.concatenate([first] * per_tile, axis=0)
    groups = tokens * held // 8
    token = iota((groups, 8, DIM), 0) * per_tile + (iota((groups, 8, DIM), 1) // held)
    tiles = tiles_ref[...].reshape(groups, 8, DIM)
    masked_ref[...] = jnp.where(token < limit[None], tiles, first[None]).reshape(groups * 8, DIM)

    nearby = feedback_ref[...] - pos * held
    number = (iota(nearby.shape, 0) * queries_n + iota(nearby.shape, 1)) * held + nearby
    far = 1e9
    key = jnp.where((nearby >= 0) & (nearby < held), number.astype(jnp.float32), far)
    ranks = ranks_ref[...].astype(jnp.float32)
    lane = iota(ranks.shape, 1)
    pay_ref[...] = jnp.zeros(pay_ref.shape, jnp.float32)
    ids = jnp.zeros((1, DIM), jnp.float32)
    slot = iota((1, DIM), 1) // EXP
    kinds = iota((NCENT, tokens), 0)
    times = iota((EXP, tokens), 1)
    wanted = iota((EXP, tokens), 0).astype(jnp.float32)
    for s in range(FB):
        best = jnp.min(key)
        key = jnp.where(key > best, key, far)
        whole = best.astype(jnp.int32)
        p = whole % held
        q = (whole // held) % queries_n
        ids = jnp.where(slot == s, q.astype(jnp.float32), ids)
        rank = jnp.sum(jnp.where(lane == q, ranks, 0.0), axis=1, keepdims=True)
        kind = clusters_ref[pl.ds(p, 1), :]
        of_token = jnp.sum(jnp.where(kind == kinds, rank, 0.0), axis=0, keepdims=True)
        chosen = jnp.where((of_token == wanted) & (times < len_ref[p]), 1.0, 0.0)
        passage = tiles_ref[pl.ds(p, tokens, stride=held), :]
        pay_ref[s * EXP:(s + 1) * EXP, :] = jnp.dot(
            chosen, passage, precision=HIGHEST, preferred_element_type=jnp.float32)
    pay_ref[ID_ROW:ID_ROW + 1, :] = ids
    for c, at in enumerate(range(0, queries_n, DIM)):
        width = min(DIM, queries_n - at)
        top = CAND_ROW + (CAP + 1) * c
        pay_ref[top:top + CAP, 0:width] = local_ref[:, at:at + width].astype(jnp.float32)
        pay_ref[top + CAP:top + CAP + 1, 0:width] = count_ref[:, at:at + width].astype(jnp.float32)


def combine_kernel(inner, outer, pos_ref, *refs):
    *pays, tokens_ref, out_ref = refs
    pos = pos_ref[0]
    inside = sum(inner)
    rows = (1 << len(outer)) * EXP
    row = iota((rows, DIM), 0)
    owner = (pos & inside) | spread(row // EXP, outer)
    col = iota((rows, DIM), 1)
    fits = (col % EXP == row % EXP) & (col < FB * EXP)
    total = jnp.zeros((rows, DIM), jnp.float32)
    for pay in pays:
        for at in range(0, pay.shape[0], pay_rows_of(pays)):
            ids = pay[at + ID_ROW:at + ID_ROW + 1, :]
            pick = jnp.where(fits & (ids == owner.astype(jnp.float32)), 1.0, 0.0)[:, :32]
            block = pay[at:at + 32, :]
            block = jnp.where(iota((32, DIM), 0) < FB * EXP, block, 0.0)
            total += jnp.dot(pick, block, precision=HIGHEST, preferred_element_type=jnp.float32)
    out_ref[0:rows, :] = total
    out_ref[rows:rows + QL, :] = tokens_ref[...]


def pay_rows_of(pays):
    return pays[0].shape[0]


def nt_dot(a, b, precision=None):
    return lax.dot_general(a, b, (((1,), (1,)), ((), ())), precision=precision, preferred_element_type=jnp.float32)


def split(x):
    high = x.astype(jnp.bfloat16)
    return high, (x - high.astype(jnp.float32)).astype(jnp.bfloat16)


def score_kernel(inner, outer, queries_n, held, tokens, n_tiles, n_pays, pos_ref, *refs):
    tile_refs = refs[:n_tiles]
    pay_refs = refs[n_tiles:n_tiles + n_pays]
    mine_ref, theirs_ref, out_ref = refs[n_tiles + n_pays:]
    pos = pos_ref[0]
    inside, outside = sum(inner), sum(outer)
    n_in, n_out = 1 << len(inner), 1 << len(outer)
    me_in = gather_bits(pos, inner)
    me_out = gather_bits(pos, outer)
    rows = n_out * EXP
    sums = mine_ref[0:rows, :] + theirs_ref[0:rows, :]
    scale = lax.rsqrt(jnp.mean(sums * sums, axis=1, keepdims=True) + 1e-05)
    order = (iota((rows, 1), 0) % EXP).astype(jnp.float32)
    weight = BETA * jnp.log((NCENT + 1.0) / (order + 1.0))
    extra = sums * (scale * weight)
    expanded = jnp.concatenate([mine_ref[rows:, :], theirs_ref[rows:, :], extra], axis=0)
    total = expanded.shape[0]
    lefts = []
    for ref in tile_refs:
        high, low = split(ref[...])
        lefts.append((high, jnp.concatenate([high, low], axis=1)))
    parts = [[] for _ in lefts]
    for at in range(0, total, 256):
        high, low = split(expanded[at:at + 256])
        twice = jnp.concatenate([high, high], axis=1)
        for i, (left, wide) in enumerate(lefts):
            similar = nt_dot(wide, twice) + nt_dot(left, low)
            groups = similar.shape[0] // 8
            parts[i].append(jnp.max(similar.reshape(groups, 8, similar.shape[1]), axis=0))
    largest = []
    for part in parts:
        top = jnp.concatenate(part, axis=1)
        step = held
        while step < 8:
            top = jnp.maximum(top, pltpu.roll(top, step, 0))
            step *= 2
        largest.append(top)
    largest = jnp.concatenate(largest, axis=0)
    col = iota((n_out, total), 1)
    of_col = jnp.where(col < n_out * QL, (col // QL) ^ me_out, (col - n_out * QL) // EXP)
    member = jnp.where(of_col == iota((n_out, total), 0), 1.0 / QL, 0.0)
    values = nt_dot(member, largest, HIGHEST)

    cands = jnp.concatenate([
        pay[at + CAND_ROW:at + CAND_ROW + 8, :]
        for pay in pay_refs for at in range(0, pay.shape[0], pay_refs[0].shape[0])
    ], axis=0)
    shape = (n_out, DIM)
    own = (pos & inside) | spread(iota(shape, 0), outer)
    slots = out_ref.shape[1]
    slot = iota((n_in * 8, slots), 1)
    entry = iota((n_in * 8, slots), 0)
    device = slot // CAP
    block = gather_bits(device, inner) ^ me_in
    same = block == entry // 8
    local = jnp.zeros((n_out, slots), jnp.float32)
    count = jnp.zeros((n_out, slots), jnp.float32)
    for c, at in enumerate(range(0, queries_n, DIM)):
        found = nt_dot(jnp.where(own - at == iota(shape, 1), 1.0, 0.0), cands, HIGHEST)
        top = (CAP + 1) * c
        pick = jnp.where(same & (entry % 8 == top + slot % CAP), 1.0, 0.0)
        local += jnp.dot(found, pick, precision=HIGHEST, preferred_element_type=jnp.float32)
        pick = jnp.where(same & (entry % 8 == top + CAP), 1.0, 0.0)
        count += jnp.dot(found, pick, precision=HIGHEST, preferred_element_type=jnp.float32)
    result = jnp.zeros((n_out, slots), jnp.float32)
    for p in range(held):
        pick = jnp.where(same & (entry % 8 == p), 1.0, 0.0)
        value = jnp.dot(values, pick, precision=HIGHEST, preferred_element_type=jnp.float32)
        result = jnp.where(local == float(p), value, result)
    slot = iota((n_out, slots), 1)
    live = ((slot % CAP).astype(jnp.float32) < count) & (((slot // CAP) & outside) == (pos & outside))
    out_ref[...] = jnp.where(live, result, 0.0)


def call(kernel, outs, *args, flops=0):
    smem = pl.BlockSpec(memory_space=pltpu.SMEM)
    vmem = pl.BlockSpec(memory_space=pltpu.VMEM)
    specs = [smem if a.ndim == 1 else vmem for a in args]
    moved = sum(a.size * 4 for a in args) + sum(o.size * 4 for o in outs)
    return pl.pallas_call(
        kernel,
        out_shape=outs if len(outs) > 1 else outs[0],
        in_specs=specs,
        out_specs=[vmem] * len(outs) if len(outs) > 1 else vmem,
        compiler_params=pltpu.CompilerParams(vmem_limit_bytes=40 * 1024 * 1024),
        cost_estimate=pl.CostEstimate(flops=flops, bytes_accessed=moved, transcendentals=0),
    )(*args)


def body(queries, passages, clusters, lengths, feedback, ranks, cand_local, cand_count):
    held, tokens, _ = passages.shape
    queries_n = feedback.shape[0]
    n_corpus = lax.axis_size("corpus")
    devices = lax.axis_size("query") * n_corpus
    masks = [1 << k for k in range(devices.bit_length() - 1)]
    inner = [1, n_corpus]
    outer = [2 * n_corpus] + [m for m in masks if m not in inner and m != 2 * n_corpus]
    n_out = 1 << len(outer)
    pos = lax.axis_index(AXES).astype(jnp.int32).reshape(1)

    def swap(x, mask):
        return lax.ppermute(x, AXES, [(i, i ^ mask) for i in range(devices)])

    def struct(rows, cols=DIM):
        return jax.ShapeDtypeStruct((rows, cols), jnp.float32)

    chunks = -(-queries_n // DIM)
    pay_rows = CAND_ROW + 8
    assert (CAP + 1) * chunks <= 8 and queries.shape[0] == 1 and 8 % held == 0
    tiles = jnp.transpose(passages, (1, 0, 2)).reshape(tokens * held, DIM)
    masked, pay = call(
        functools.partial(pairs_kernel, queries_n, held, tokens),
        [struct(tokens * held), struct(pay_rows)],
        pos, lengths, tiles, clusters, feedback.T, ranks.T, cand_local.T, cand_count.T,
    )
    blocks, pays = [masked], [pay]
    for mask in inner:
        blocks = blocks + [swap(b, mask) for b in blocks]
        joined = pays[0] if len(pays) == 1 else jnp.concatenate(pays, axis=0)
        pays = pays + [swap(joined, mask)]
    send = call(functools.partial(combine_kernel, inner, outer), [struct(n_out * EXP + QL)], pos, *pays, queries[0])
    rows = n_out * EXP
    for mask in outer[:-1]:
        came = swap(send, mask)
        send = jnp.concatenate([send[:rows] + came[:rows], send[rows:], came[rows:]], axis=0)
    came = swap(send, outer[-1])
    table = call(
        functools.partial(score_kernel, inner, outer, queries_n, held, tokens, len(blocks), len(pays)),
        [struct(n_out, devices * CAP)],
        pos, *blocks, *pays, send, came,
        flops=2 * 3 * n_out * (QL + EXP) * len(blocks) * held * tokens * DIM,
    )
    for mask in reversed(outer):
        table = table + swap(table, mask)
    mine = sum(jnp.where((pos[0] & mask) != 0, 1 << k, 0) for k, mask in enumerate(outer))
    return lax.dynamic_slice(table, (mine, 0), (1, devices * CAP))


def solution(mesh):
    in_specs = (
        P(AXES, None, None),
        P(AXES, None, None),
        P(AXES, None),
        P(AXES),
        P(),
        P(),
        P(None, AXES),
        P(None, AXES),
    )
    return jax.shard_map(body, mesh=mesh, in_specs=in_specs, out_specs=P(AXES, None), check_vma=False)
```

```python
import functools

import jax
import jax.numpy as jnp
from jax import lax
from jax.experimental import pallas as pl
from jax.experimental.pallas import tpu as pltpu
from jax.sharding import PartitionSpec as P

DIM = 128
QL = 32
NCENT = 24
EXP = 10
CAP = 2
FB = 3
BETA = 0.5
AXES = ("query", "corpus")
ID_ROW = 31
CAND_ROW = 32
HIGHEST = lax.Precision.HIGHEST


def iota(shape, axis):
    return lax.broadcasted_iota(jnp.int32, shape, axis)


def spread(index, masks):
    total = 0
    for k, mask in enumerate(masks):
        total = total | (((index >> k) & 1) * mask)
    return total


def gather_bits(device, masks):
    total = 0
    for k, mask in enumerate(masks):
        total = total | (jnp.where((device & mask) != 0, 1, 0) << k)
    return total


def pairs_kernel(queries_n, held, tokens, pos_ref, len_ref, tiles_ref, clusters_ref, feedback_ref, ranks_ref,
                 local_ref, count_ref, masked_ref, pay_ref):
    pos = pos_ref[0]
    per_tile = 8 // held
    row = iota((8, DIM), 0)
    limit = jnp.zeros((8, DIM), jnp.int32)
    for p in range(held):
        limit = jnp.where(row % held == p, len_ref[p], limit)
    first = tiles_ref[0:held, :]
    first = jnp.concatenate([first] * per_tile, axis=0)
    groups = tokens * held // 8
    token = iota((groups, 8, DIM), 0) * per_tile + (iota((groups, 8, DIM), 1) // held)
    tiles = tiles_ref[...].reshape(groups, 8, DIM)
    masked_ref[...] = jnp.where(token < limit[None], tiles, first[None]).reshape(groups * 8, DIM)

    nearby = feedback_ref[...] - pos * held
    number = (iota(nearby.shape, 0) * queries_n + iota(nearby.shape, 1)) * held + nearby
    far = 1e9
    key = jnp.where((nearby >= 0) & (nearby < held), number.astype(jnp.float32), far)
    ranks = ranks_ref[...].astype(jnp.float32)
    lane = iota(ranks.shape, 1)
    pay_ref[...] = jnp.zeros(pay_ref.shape, jnp.float32)
    ids = jnp.zeros((1, DIM), jnp.float32)
    slot = iota((1, DIM), 1) // EXP
    kinds = iota((NCENT, tokens), 0)
    times = iota((EXP, tokens), 1)
    wanted = iota((EXP, tokens), 0).astype(jnp.float32)
    for s in range(FB):
        best = jnp.min(key)
        key = jnp.where(key > best, key, far)
        whole = best.astype(jnp.int32)
        p = whole % held
        q = (whole // held) % queries_n
        ids = jnp.where(slot == s, q.astype(jnp.float32), ids)
        rank = jnp.sum(jnp.where(lane == q, ranks, 0.0), axis=1, keepdims=True)
        kind = clusters_ref[pl.ds(p, 1), :]
        of_token = jnp.sum(jnp.where(kind == kinds, rank, 0.0), axis=0, keepdims=True)
        chosen = jnp.where((of_token == wanted) & (times < len_ref[p]), 1.0, 0.0)
        passage = tiles_ref[pl.ds(p, tokens, stride=held), :]
        pay_ref[s * EXP:(s + 1) * EXP, :] = jnp.dot(
            chosen, passage, precision=HIGHEST, preferred_element_type=jnp.float32)
    pay_ref[ID_ROW:ID_ROW + 1, :] = ids
    for c, at in enumerate(range(0, queries_n, DIM)):
        width = min(DIM, queries_n - at)
        top = CAND_ROW + (CAP + 1) * c
        pay_ref[top:top + CAP, 0:width] = local_ref[:, at:at + width].astype(jnp.float32)
        pay_ref[top + CAP:top + CAP + 1, 0:width] = count_ref[:, at:at + width].astype(jnp.float32)


def combine_kernel(inner, outer, pos_ref, *refs):
    *pays, out_ref = refs
    pos = pos_ref[0]
    inside = sum(inner)
    rows = (1 << len(outer)) * EXP
    row = iota((rows, DIM), 0)
    owner = (pos & inside) | spread(row // EXP, outer)
    col = iota((rows, DIM), 1)
    fits = (col % EXP == row % EXP) & (col < FB * EXP)
    total = jnp.zeros((rows, DIM), jnp.float32)
    for pay in pays:
        for at in range(0, pay.shape[0], pay_rows_of(pays)):
            ids = pay[at + ID_ROW:at + ID_ROW + 1, :]
            pick = jnp.where(fits & (ids == owner.astype(jnp.float32)), 1.0, 0.0)[:, :32]
            block = pay[at:at + 32, :]
            block = jnp.where(iota((32, DIM), 0) < FB * EXP, block, 0.0)
            total += jnp.dot(pick, block, precision=HIGHEST, preferred_element_type=jnp.float32)
    out_ref[...] = total


def pay_rows_of(pays):
    return pays[0].shape[0]


def nt_dot(a, b, precision=None):
    return lax.dot_general(a, b, (((1,), (1,)), ((), ())), precision=precision, preferred_element_type=jnp.float32)


def split(x):
    high = x.astype(jnp.bfloat16)
    return high, (x - high.astype(jnp.float32)).astype(jnp.bfloat16)


def score_kernel(inner, outer, queries_n, held, tokens, n_tiles, n_pays, n_asks, pos_ref, *refs):
    tile_refs = refs[:n_tiles]
    pay_refs = refs[n_tiles:n_tiles + n_pays]
    ask_refs = refs[n_tiles + n_pays:n_tiles + n_pays + n_asks]
    mine_ref, theirs_ref, out_ref = refs[n_tiles + n_pays + n_asks:]
    pos = pos_ref[0]
    inside, outside = sum(inner), sum(outer)
    n_in, n_out = 1 << len(inner), 1 << len(outer)
    me_in = gather_bits(pos, inner)
    me_out = gather_bits(pos, outer)
    sums = mine_ref[...] + theirs_ref[...]
    scale = lax.rsqrt(jnp.mean(sums * sums, axis=1, keepdims=True) + 1e-05)
    order = (iota((n_out * EXP, 1), 0) % EXP).astype(jnp.float32)
    weight = BETA * jnp.log((NCENT + 1.0) / (order + 1.0))
    extra = sums * (scale * weight)
    expanded = jnp.concatenate([ask[...] for ask in ask_refs] + [extra], axis=0)
    total = expanded.shape[0]
    lefts = []
    for ref in tile_refs:
        high, low = split(ref[...])
        lefts.append((high, jnp.concatenate([high, low], axis=1)))
    parts = [[] for _ in lefts]
    for at in range(0, total, 256):
        high, low = split(expanded[at:at + 256])
        twice = jnp.concatenate([high, high], axis=1)
        for i, (left, wide) in enumerate(lefts):
            similar = nt_dot(wide, twice) + nt_dot(left, low)
            groups = similar.shape[0] // 8
            parts[i].append(jnp.max(similar.reshape(groups, 8, similar.shape[1]), axis=0))
    largest = []
    for part in parts:
        top = jnp.concatenate(part, axis=1)
        step = held
        while step < 8:
            top = jnp.maximum(top, pltpu.roll(top, step, 0))
            step *= 2
        largest.append(top)
    largest = jnp.concatenate(largest, axis=0)
    col = iota((n_out, total), 1)
    of_col = jnp.where(col < n_out * QL, (col // QL) ^ me_out, (col - n_out * QL) // EXP)
    member = jnp.where(of_col == iota((n_out, total), 0), 1.0 / QL, 0.0)
    values = nt_dot(member, largest, HIGHEST)

    cands = jnp.concatenate([
        pay[at + CAND_ROW:at + CAND_ROW + 8, :]
        for pay in pay_refs for at in range(0, pay.shape[0], pay_refs[0].shape[0])
    ], axis=0)
    shape = (n_out, DIM)
    own = (pos & inside) | spread(iota(shape, 0), outer)
    slots = out_ref.shape[1]
    slot = iota((n_in * 8, slots), 1)
    entry = iota((n_in * 8, slots), 0)
    device = slot // CAP
    block = gather_bits(device, inner) ^ me_in
    same = block == entry // 8
    local = jnp.zeros((n_out, slots), jnp.float32)
    count = jnp.zeros((n_out, slots), jnp.float32)
    for c, at in enumerate(range(0, queries_n, DIM)):
        found = nt_dot(jnp.where(own - at == iota(shape, 1), 1.0, 0.0), cands, HIGHEST)
        top = (CAP + 1) * c
        pick = jnp.where(same & (entry % 8 == top + slot % CAP), 1.0, 0.0)
        local += jnp.dot(found, pick, precision=HIGHEST, preferred_element_type=jnp.float32)
        pick = jnp.where(same & (entry % 8 == top + CAP), 1.0, 0.0)
        count += jnp.dot(found, pick, precision=HIGHEST, preferred_element_type=jnp.float32)
    result = jnp.zeros((n_out, slots), jnp.float32)
    for p in range(held):
        pick = jnp.where(same & (entry % 8 == p), 1.0, 0.0)
        value = jnp.dot(values, pick, precision=HIGHEST, preferred_element_type=jnp.float32)
        result = jnp.where(local == float(p), value, result)
    slot = iota((n_out, slots), 1)
    live = ((slot % CAP).astype(jnp.float32) < count) & (((slot // CAP) & outside) == (pos & outside))
    out_ref[...] = jnp.where(live, result, 0.0)


def call(kernel, outs, *args, flops=0):
    smem = pl.BlockSpec(memory_space=pltpu.SMEM)
    vmem = pl.BlockSpec(memory_space=pltpu.VMEM)
    specs = [smem if a.ndim == 1 else vmem for a in args]
    moved = sum(a.size * 4 for a in args) + sum(o.size * 4 for o in outs)
    return pl.pallas_call(
        kernel,
        out_shape=outs if len(outs) > 1 else outs[0],
        in_specs=specs,
        out_specs=[vmem] * len(outs) if len(outs) > 1 else vmem,
        compiler_params=pltpu.CompilerParams(vmem_limit_bytes=40 * 1024 * 1024),
        cost_estimate=pl.CostEstimate(flops=flops, bytes_accessed=moved, transcendentals=0),
    )(*args)


def body(queries, passages, clusters, lengths, feedback, ranks, cand_local, cand_count):
    held, tokens, _ = passages.shape
    queries_n = feedback.shape[0]
    n_corpus = lax.axis_size("corpus")
    devices = lax.axis_size("query") * n_corpus
    masks = [1 << k for k in range(devices.bit_length() - 1)]
    inner = [n_corpus, 1]
    outer = [m for m in reversed(masks) if m not in inner and m != 2 * n_corpus] + [2 * n_corpus]
    n_out = 1 << len(outer)
    pos = lax.axis_index(AXES).astype(jnp.int32).reshape(1)

    def swap(x, mask):
        return lax.ppermute(x, AXES, [(i, i ^ mask) for i in range(devices)])

    def struct(rows, cols=DIM):
        return jax.ShapeDtypeStruct((rows, cols), jnp.float32)

    chunks = -(-queries_n // DIM)
    pay_rows = CAND_ROW + 8
    assert (CAP + 1) * chunks <= 8 and queries.shape[0] == 1 and 8 % held == 0
    tiles = jnp.transpose(passages, (1, 0, 2)).reshape(tokens * held, DIM)
    masked, pay = call(
        functools.partial(pairs_kernel, queries_n, held, tokens),
        [struct(tokens * held), struct(pay_rows)],
        pos, lengths, tiles, clusters, feedback.T, ranks.T, cand_local.T, cand_count.T,
    )
    asks = [queries[0]]

    def ask(mask):
        joined = asks[0] if len(asks) == 1 else jnp.concatenate(asks, axis=0)
        return asks + [swap(joined, mask)]

    def together(*xs):
        return lax.optimization_barrier(xs)

    asks = ask(outer[0])
    pays = [pay, swap(pay, inner[0])]
    masked, _ = together(masked, pays)
    far = swap(masked, inner[0])
    pays = pays + [swap(jnp.concatenate(pays, axis=0), inner[1])]
    sums = call(functools.partial(combine_kernel, inner, outer), [struct(n_out * EXP)], pos, *pays)
    for mask, coming in zip(outer[:-1], outer[1:]):
        asks = ask(coming)
        sums = sums + swap(sums, mask)
    masked, far, asks, _ = together(masked, far, asks, sums)
    blocks = [masked, far, swap(masked, inner[1]), swap(far, inner[1])]
    came = swap(sums, outer[-1])
    table = call(
        functools.partial(score_kernel, inner, outer, queries_n, held, tokens, len(blocks), len(pays), len(asks)),
        [struct(n_out, devices * CAP)],
        pos, *blocks, *pays, *asks, sums, came,
        flops=2 * 3 * n_out * (QL + EXP) * len(blocks) * held * tokens * DIM,
    )
    for mask in reversed(outer):
        table = table + swap(table, mask)
    mine = sum(jnp.where((pos[0] & mask) != 0, 1 << k, 0) for k, mask in enumerate(outer))
    return lax.dynamic_slice(table, (mine, 0), (1, devices * CAP))


def solution(mesh):
    in_specs = (
        P(AXES, None, None),
        P(AXES, None, None),
        P(AXES, None),
        P(AXES),
        P(),
        P(),
        P(None, AXES),
        P(None, AXES),
    )
    return jax.shard_map(body, mesh=mesh, in_specs=in_specs, out_specs=P(AXES, None), check_vma=False)
```

```python
import functools

import jax
import jax.numpy as jnp
from jax import lax
from jax.experimental import pallas as pl
from jax.experimental.pallas import tpu as pltpu
from jax.sharding import PartitionSpec as P

DIM = 128
QL = 32
NCENT = 24
EXP = 10
CAP = 2
FB = 3
BETA = 0.5
AXES = ("query", "corpus")
ID_ROW = 31
CAND_ROW = 32
ASK_ROW = 40
HIGHEST = lax.Precision.HIGHEST


def iota(shape, axis):
    return lax.broadcasted_iota(jnp.int32, shape, axis)


def spread(index, masks):
    total = 0
    for k, mask in enumerate(masks):
        total = total | (((index >> k) & 1) * mask)
    return total


def gather_bits(device, masks):
    total = 0
    for k, mask in enumerate(masks):
        total = total | (jnp.where((device & mask) != 0, 1, 0) << k)
    return total


def pairs_kernel(queries_n, held, tokens, pos_ref, *refs):
    sources, (masked_ref, pay_ref) = refs[:7], refs[7:9]
    landed, sems = refs[9:16], refs[16]
    copies = [pltpu.make_async_copy(a, b, sems.at[k]) for k, (a, b) in enumerate(zip(sources, landed))]
    for copy in copies:
        copy.start()
    for copy in copies:
        copy.wait()
    len_ref, tiles_ref, clusters_ref, feedback_ref, ranks_ref, local_ref, count_ref = landed
    pos = pos_ref[0]
    per_tile = 8 // held
    row = iota((8, DIM), 0)
    limit = jnp.zeros((8, DIM), jnp.int32)
    for p in range(held):
        limit = jnp.where(row % held == p, len_ref[p], limit)
    first = tiles_ref[0:held, :]
    first = jnp.concatenate([first] * per_tile, axis=0)
    groups = tokens * held // 8
    token = iota((groups, 8, DIM), 0) * per_tile + (iota((groups, 8, DIM), 1) // held)
    tiles = tiles_ref[...].reshape(groups, 8, DIM)
    masked_ref[...] = jnp.where(token < limit[None], tiles, first[None]).reshape(groups * 8, DIM)

    nearby = feedback_ref[...] - pos * held
    number = (iota(nearby.shape, 0) * queries_n + iota(nearby.shape, 1)) * held + nearby
    far = 1e9
    key = jnp.where((nearby >= 0) & (nearby < held), number.astype(jnp.float32), far)
    ranks = ranks_ref[...].astype(jnp.float32)
    lane = iota(ranks.shape, 1)
    pay_ref[:ASK_ROW, :] = jnp.zeros((ASK_ROW, DIM), jnp.float32)
    ids = jnp.zeros((1, DIM), jnp.float32)
    slot = iota((1, DIM), 1) // EXP
    kinds = iota((NCENT, tokens), 0)
    times = iota((EXP, tokens), 1)
    wanted = iota((EXP, tokens), 0).astype(jnp.float32)
    for s in range(FB):
        best = jnp.min(key)
        key = jnp.where(key > best, key, far)
        whole = best.astype(jnp.int32)
        p = whole % held
        q = (whole // held) % queries_n
        ids = jnp.where(slot == s, q.astype(jnp.float32), ids)
        rank = jnp.sum(jnp.where(lane == q, ranks, 0.0), axis=1, keepdims=True)
        kind = clusters_ref[pl.ds(p, 1), :]
        of_token = jnp.sum(jnp.where(kind == kinds, rank, 0.0), axis=0, keepdims=True)
        chosen = jnp.where((of_token == wanted) & (times < len_ref[p]), 1.0, 0.0)
        passage = tiles_ref[pl.ds(p, tokens, stride=held), :]
        pay_ref[s * EXP:(s + 1) * EXP, :] = jnp.dot(
            chosen, passage, precision=HIGHEST, preferred_element_type=jnp.float32)
    pay_ref[ID_ROW:ID_ROW + 1, :] = ids
    for c, at in enumerate(range(0, queries_n, DIM)):
        width = min(DIM, queries_n - at)
        top = CAND_ROW + (CAP + 1) * c
        pay_ref[top:top + CAP, 0:width] = local_ref[:, at:at + width].astype(jnp.float32)
        pay_ref[top + CAP:top + CAP + 1, 0:width] = count_ref[:, at:at + width].astype(jnp.float32)


def combine_kernel(side, outer, pos_ref, *refs):
    *pays, keep_ref, send_ref = refs
    pos = pos_ref[0]
    half = (1 << len(outer)) * EXP
    rows = 2 * half
    row = iota((rows, DIM), 0)
    owner = ((pos ^ ((row // half) * side)) & (1 | side)) | spread(row % half // EXP, outer)
    owner = owner.astype(jnp.float32)
    places = [(pay, 0) for pay in pays]
    total = jnp.zeros((rows, DIM), jnp.float32)
    for group in range(0, len(places), 8):
        some = places[group:group + 8]
        ids = jnp.concatenate([pay[at + ID_ROW:at + ID_ROW + 1, :CAND_ROW] for pay, at in some], axis=1)
        col = iota((rows, ids.shape[1]), 1) % CAND_ROW
        pick = (col % EXP == row[:, :1] % EXP) & (col < FB * EXP) & (ids == owner[:, :1])
        pick = jnp.where(pick, 1.0, 0.0).astype(jnp.bfloat16)
        block = jnp.concatenate([pay[at:at + CAND_ROW, :] for pay, at in some], axis=0)
        high, low = split(block)
        rest = (block - high.astype(jnp.float32) - low.astype(jnp.float32)).astype(jnp.bfloat16)
        for piece in (rest, low, high):
            total += jnp.dot(pick, piece, preferred_element_type=jnp.float32)
    for ref, sums in ((keep_ref, total[:rows // 2]), (send_ref, total[rows // 2:])):
        ref[:rows // 2, :] = sums
        ref[rows // 2:rows // 2 + 8, :] = pays[0][CAND_ROW:ASK_ROW, :]
        ref[rows // 2 + 8:, :] = pays[-1][CAND_ROW:ASK_ROW, :]


def nt_dot(a, b, precision=None):
    return lax.dot_general(a, b, (((1,), (1,)), ((), ())), precision=precision, preferred_element_type=jnp.float32)


def split(x):
    high = x.astype(jnp.bfloat16)
    return high, (x - high.astype(jnp.float32)).astype(jnp.bfloat16)


def score_kernel(side, outer, asking, queries_n, held, n_tiles, n_asks, pos_ref, *refs):
    tile_refs, ask_refs = refs[:n_tiles], refs[n_tiles:n_tiles + n_asks]
    keep_ref, from_side_ref, mine_ref, theirs_ref, out_ref = refs[n_tiles + n_asks:]
    pos = pos_ref[0]
    n_in, n_out = 4, 1 << len(outer)
    me_out = gather_bits(pos, outer)
    half = n_out * EXP
    sums = mine_ref[...] + theirs_ref[...]
    scale = lax.rsqrt(jnp.mean(sums * sums, axis=1, keepdims=True) + 1e-05)
    order = (iota((half, 1), 0) % EXP).astype(jnp.float32)
    weight = BETA * jnp.log((NCENT + 1.0) / (order + 1.0))
    extra = sums * (scale * weight)
    expanded = jnp.concatenate([ask[...] for ask in ask_refs] + [extra], axis=0)
    total = expanded.shape[0]
    lefts = []
    for ref in tile_refs:
        high, low = split(ref[...])
        lefts.append((high, jnp.concatenate([high, low], axis=1)))
    parts = [[] for _ in lefts]
    for at in range(0, total, 256):
        high, low = split(expanded[at:at + 256])
        twice = jnp.concatenate([high, high], axis=1)
        for i, (left, wide) in enumerate(lefts):
            similar = nt_dot(wide, twice) + nt_dot(left, low)
            groups = similar.shape[0] // 8
            parts[i].append(jnp.max(similar.reshape(groups, 8, similar.shape[1]), axis=0))
    largest = []
    for part in parts:
        top = jnp.concatenate(part, axis=1)
        step = held
        while step < 8:
            top = jnp.maximum(top, pltpu.roll(top, step, 0))
            step *= 2
        largest.append(top)
    largest = jnp.concatenate(largest, axis=0)
    col = iota((n_out, total), 1)
    of_ask = gather_bits(spread(col // QL, asking), outer) ^ me_out
    of_col = jnp.where(col < n_out * QL, of_ask, (col - n_out * QL) // EXP)
    member = jnp.where(of_col == iota((n_out, total), 0), 1.0 / QL, 0.0)
    values = nt_dot(member, largest, HIGHEST)

    cands = jnp.concatenate([keep_ref[half:, :], from_side_ref[half:, :]], axis=0)
    own = (pos & ~sum(outer)) | spread(iota((n_out, DIM), 0), outer)
    slots = out_ref.shape[1]
    device = iota((n_in * 8, slots), 1) // CAP
    which = iota((n_in * 8, slots), 1) % CAP
    entry = iota((n_in * 8, slots), 0)

    def at_device(steps):
        place = jnp.zeros((n_in * 8, slots), jnp.int32)
        for i, away in enumerate(steps):
            place = jnp.where(entry // 8 == i, pos ^ away, place)
        return place == device

    same = at_device([0, 1, side, side | 1])
    local = jnp.zeros((n_out, slots), jnp.float32)
    count = jnp.zeros((n_out, slots), jnp.float32)
    for c, at in enumerate(range(0, queries_n, DIM)):
        found = nt_dot(jnp.where(own - at == iota((n_out, DIM), 1), 1.0, 0.0), cands, HIGHEST)
        top = (CAP + 1) * c
        pick = jnp.where(same & (entry % 8 == top + which), 1.0, 0.0)
        local += jnp.dot(found, pick, precision=HIGHEST, preferred_element_type=jnp.float32)
        pick = jnp.where(same & (entry % 8 == top + CAP), 1.0, 0.0)
        count += jnp.dot(found, pick, precision=HIGHEST, preferred_element_type=jnp.float32)
    same = at_device([0, side, 1, side | 1])
    result = jnp.zeros((n_out, slots), jnp.float32)
    for p in range(held):
        pick = jnp.where(same & (entry % 8 == p), 1.0, 0.0)
        value = jnp.dot(values, pick, precision=HIGHEST, preferred_element_type=jnp.float32)
        result = jnp.where(local == float(p), value, result)
    out_ref[...] = jnp.where((iota((n_out, slots), 1) % CAP).astype(jnp.float32) < count, result, 0.0)


def call(kernel, outs, *args, copied=False):
    smem = pl.BlockSpec(memory_space=pltpu.SMEM)
    vmem = pl.BlockSpec(memory_space=pltpu.VMEM)
    specs = [smem if a.ndim == 1 else vmem for a in args]
    scratch = []
    if copied:
        specs[1:] = [pl.BlockSpec(memory_space=pltpu.HBM)] * (len(args) - 1)
        scratch = [(pltpu.SMEM if a.ndim == 1 else pltpu.VMEM)(a.shape, a.dtype) for a in args[1:]]
        scratch += [pltpu.SemaphoreType.DMA((len(args) - 1,))]
        args = args[:1] + tuple(pltpu.with_memory_space_constraint(a, pltpu.HBM) for a in args[1:])
    return pl.pallas_call(
        kernel,
        out_shape=[pltpu.VMEM(o.shape, o.dtype) for o in outs] if len(outs) > 1 else outs[0],
        in_specs=specs,
        out_specs=[vmem] * len(outs) if len(outs) > 1 else vmem,
        scratch_shapes=scratch,
        compiler_params=pltpu.CompilerParams(vmem_limit_bytes=24 * 1024 * 1024),
    )(*args)


def body(queries, passages, clusters, lengths, feedback, ranks, cand_local, cand_count):
    held, tokens, _ = passages.shape
    queries_n = feedback.shape[0]
    n_corpus = lax.axis_size("corpus")
    devices = lax.axis_size("query") * n_corpus
    side, last = n_corpus, 2 * n_corpus
    masks = [1 << k for k in range(devices.bit_length() - 1)]
    outer = [m for m in reversed(masks) if 1 < m < n_corpus] + [m for m in masks if m >= last]
    asking = outer[1:] + outer[:1]
    n_out = 1 << len(outer)
    pos = lax.axis_index(AXES).astype(jnp.int32).reshape(1)

    def swap(x, mask):
        return lax.ppermute(x, AXES, [(i, i ^ mask) for i in range(devices)])

    def struct(rows, cols=DIM):
        return jax.ShapeDtypeStruct((rows, cols), jnp.float32)

    chunks = -(-queries_n // DIM)
    pay_rows = ASK_ROW
    assert (CAP + 1) * chunks <= 8 and queries.shape[0] == 1 and 8 % held == 0
    tiles = jnp.transpose(passages, (1, 0, 2)).reshape(tokens * held, DIM)
    masked, pay = call(
        functools.partial(pairs_kernel, queries_n, held, tokens),
        [struct(tokens * held), struct(pay_rows)],
        pos, lengths, tiles, clusters, feedback.T, ranks.T, cand_local.T, cand_count.T, copied=True,
    )
    def together(*xs):
        return lax.optimization_barrier(xs)

    def joined(xs):
        return xs[0] if len(xs) == 1 else jnp.concatenate(xs, axis=0)

    beside = swap(pay, 1)
    half = n_out * EXP
    keep, send = call(functools.partial(combine_kernel, side, outer), [struct(half + 16)] * 2, pos, pay, beside)
    from_side = swap(send, side)
    sums = keep[:half] + from_side[:half]
    asks = [queries[0]]
    for mask in asking:
        asks = asks + [swap(joined(asks), mask)]
    masked, _ = lax.optimization_barrier((masked, asks[1]))
    far = swap(masked, side)
    for mask in outer[:-1]:
        sums = sums + swap(sums, mask)
    far, sums, asks = lax.optimization_barrier((far, sums, asks))
    came = swap(sums, outer[-1])
    tiles = [masked, far]
    tiles = tiles + [swap(t, 1) for t in tiles]
    table = call(
        functools.partial(score_kernel, side, outer, asking, queries_n, held, len(tiles), len(asks)),
        [struct(n_out, devices * CAP)],
        pos, *tiles, *asks, keep, from_side, sums, came,
    )
    for mask in reversed(outer):
        table = table + swap(table, mask)
    mine = sum(jnp.where((pos[0] & mask) != 0, 1 << k, 0) for k, mask in enumerate(outer))
    return lax.dynamic_slice(table, (mine, 0), (1, devices * CAP))


def solution(mesh):
    in_specs = (
        P(AXES, None, None),
        P(AXES, None, None),
        P(AXES, None),
        P(AXES),
        P(),
        P(),
        P(None, AXES),
        P(None, AXES),
    )
    return jax.shard_map(body, mesh=mesh, in_specs=in_specs, out_specs=P(AXES, None), check_vma=False)
```

```python
import functools

import jax
import jax.numpy as jnp
from jax import lax
from jax.experimental import pallas as pl
from jax.experimental.pallas import tpu as pltpu
from jax.sharding import PartitionSpec as P

DIM = 128
QL = 32
NCENT = 24
EXP = 10
CAP = 2
FB = 3
BETA = 0.5
AXES = ("query", "corpus")
ID_ROW = 31
CAND_ROW = 32
ASK_ROW = 40
HIGHEST = lax.Precision.HIGHEST


def iota(shape, axis):
    return lax.broadcasted_iota(jnp.int32, shape, axis)


def spread(index, masks):
    total = 0
    for k, mask in enumerate(masks):
        total = total | (((index >> k) & 1) * mask)
    return total


def gather_bits(device, masks):
    total = 0
    for k, mask in enumerate(masks):
        total = total | (jnp.where((device & mask) != 0, 1, 0) << k)
    return total


def pairs_kernel(queries_n, held, tokens, pos_ref, *refs):
    sources, (masked_ref, pay_ref) = refs[:7], refs[7:9]
    landed, sems = refs[9:16], refs[16]
    copies = [pltpu.make_async_copy(a, b, sems.at[k]) for k, (a, b) in enumerate(zip(sources, landed))]
    for copy in copies:
        copy.start()
    for copy in copies:
        copy.wait()
    len_ref, tiles_ref, clusters_ref, feedback_ref, ranks_ref, local_ref, count_ref = landed
    pos = pos_ref[0]
    per_tile = 8 // held
    row = iota((8, DIM), 0)
    limit = jnp.zeros((8, DIM), jnp.int32)
    for p in range(held):
        limit = jnp.where(row % held == p, len_ref[p], limit)
    first = tiles_ref[0:held, :]
    first = jnp.concatenate([first] * per_tile, axis=0)
    groups = tokens * held // 8
    token = iota((groups, 8, DIM), 0) * per_tile + (iota((groups, 8, DIM), 1) // held)
    tiles = tiles_ref[...].reshape(groups, 8, DIM)
    masked_ref[...] = jnp.where(token < limit[None], tiles, first[None]).reshape(groups * 8, DIM)

    nearby = feedback_ref[...] - pos * held
    number = (iota(nearby.shape, 0) * queries_n + iota(nearby.shape, 1)) * held + nearby
    far = 1e9
    key = jnp.where((nearby >= 0) & (nearby < held), number.astype(jnp.float32), far)
    ranks = ranks_ref[...].astype(jnp.float32)
    lane = iota(ranks.shape, 1)
    pay_ref[:ASK_ROW, :] = jnp.zeros((ASK_ROW, DIM), jnp.float32)
    ids = jnp.zeros((1, DIM), jnp.float32)
    slot = iota((1, DIM), 1) // EXP
    kinds = iota((NCENT, tokens), 0)
    times = iota((EXP, tokens), 1)
    wanted = iota((EXP, tokens), 0).astype(jnp.float32)
    for s in range(FB):
        best = jnp.min(key)
        key = jnp.where(key > best, key, far)
        whole = best.astype(jnp.int32)
        p = whole % held
        q = (whole // held) % queries_n
        ids = jnp.where(slot == s, q.astype(jnp.float32), ids)
        rank = jnp.sum(jnp.where(lane == q, ranks, 0.0), axis=1, keepdims=True)
        kind = clusters_ref[pl.ds(p, 1), :]
        of_token = jnp.sum(jnp.where(kind == kinds, rank, 0.0), axis=0, keepdims=True)
        chosen = jnp.where((of_token == wanted) & (times < len_ref[p]), 1.0, 0.0)
        passage = tiles_ref[pl.ds(p, tokens, stride=held), :]
        pieces = jnp.dot(chosen.astype(jnp.bfloat16), jnp.concatenate(thirds(passage), axis=1),
                         preferred_element_type=jnp.float32)
        pay_ref[s * EXP:(s + 1) * EXP, :] = pieces[:, 2 * DIM:] + pieces[:, DIM:2 * DIM] + pieces[:, :DIM]
    pay_ref[ID_ROW:ID_ROW + 1, :] = ids
    for c, at in enumerate(range(0, queries_n, DIM)):
        width = min(DIM, queries_n - at)
        top = CAND_ROW + (CAP + 1) * c
        pay_ref[top:top + CAP, 0:width] = local_ref[:, at:at + width].astype(jnp.float32)
        pay_ref[top + CAP:top + CAP + 1, 0:width] = count_ref[:, at:at + width].astype(jnp.float32)


def combine_kernel(side, outer, pos_ref, *refs):
    *pays, keep_ref, send_ref = refs
    pos = pos_ref[0]
    half = (1 << len(outer)) * EXP
    rows = 2 * half
    row = iota((rows, DIM), 0)
    owner = ((pos ^ ((row // half) * side)) & (1 | side)) | spread(row % half // EXP, outer)
    owner = owner.astype(jnp.float32)
    places = [(pay, 0) for pay in pays]
    total = jnp.zeros((rows, DIM), jnp.float32)
    for group in range(0, len(places), 8):
        some = places[group:group + 8]
        ids = jnp.concatenate([pay[at + ID_ROW:at + ID_ROW + 1, :CAND_ROW] for pay, at in some], axis=1)
        col = iota((rows, ids.shape[1]), 1) % CAND_ROW
        pick = (col % EXP == row[:, :1] % EXP) & (col < FB * EXP) & (ids == owner[:, :1])
        pick = jnp.where(pick, 1.0, 0.0).astype(jnp.bfloat16)
        block = jnp.concatenate([pay[at:at + CAND_ROW, :] for pay, at in some], axis=0)
        for piece in thirds(block)[::-1]:
            total += jnp.dot(pick, piece, preferred_element_type=jnp.float32)
    for ref, sums in ((keep_ref, total[:rows // 2]), (send_ref, total[rows // 2:])):
        ref[:rows // 2, :] = sums
        ref[rows // 2:rows // 2 + 8, :] = pays[0][CAND_ROW:ASK_ROW, :]
        ref[rows // 2 + 8:, :] = pays[-1][CAND_ROW:ASK_ROW, :]


def nt_dot(a, b, precision=None):
    return lax.dot_general(a, b, (((1,), (1,)), ((), ())), precision=precision, preferred_element_type=jnp.float32)


def thirds(x):
    high, low = split(x)
    return high, low, (x - high.astype(jnp.float32) - low.astype(jnp.float32)).astype(jnp.bfloat16)


def split(x):
    high = x.astype(jnp.bfloat16)
    return high, (x - high.astype(jnp.float32)).astype(jnp.bfloat16)


def at_steps(pos, steps, device, entry):
    place = jnp.zeros(entry.shape, jnp.int32)
    for i, away in enumerate(steps):
        place = jnp.where(entry // 8 == i, pos ^ away, place)
    return place == device


def largest_rows(parts, held):
    rows = []
    for top in parts:
        step = held
        while step < 8:
            top = jnp.maximum(top, pltpu.roll(top, step, 0))
            step *= 2
        rows.append(top)
    return jnp.concatenate(rows, axis=0)


def over_tokens(similar):
    return jnp.max(similar.reshape(similar.shape[0] // 8, 8, similar.shape[1]), axis=0)


def match_kernel(side, outer, asking, queries_n, held, n_tiles, n_asks, pos_ref, *refs):
    tile_refs, ask_refs = refs[:n_tiles], refs[n_tiles:n_tiles + n_asks]
    keep_ref, from_side_ref = refs[n_tiles + n_asks:n_tiles + n_asks + 2]
    *wide_refs, values_ref, chosen_ref = refs[n_tiles + n_asks + 2:]
    pos = pos_ref[0]
    n_out = 1 << len(outer)
    me_out = gather_bits(pos, outer)
    half = n_out * EXP
    tokens = jnp.concatenate([ask[...] for ask in ask_refs], axis=0)
    total = tokens.shape[0]
    lefts = []
    for ref, wide_ref in zip(tile_refs, wide_refs):
        high, low = split(ref[...])
        wide = jnp.concatenate([high, low], axis=1)
        wide_ref[...] = wide
        lefts.append((high, wide))
    parts = [[] for _ in lefts]
    for at in range(0, total, 256):
        high, low = split(tokens[at:at + 256])
        twice = jnp.concatenate([high, high], axis=1)
        for i, (left, wide) in enumerate(lefts):
            parts[i].append(over_tokens(nt_dot(wide, twice) + nt_dot(left, low)))
    largest = largest_rows([jnp.concatenate(part, axis=1) for part in parts], held)
    of_col = gather_bits(spread(iota((n_out, total), 1) // QL, asking), outer) ^ me_out
    member = jnp.where(of_col == iota((n_out, total), 0), 1.0 / QL, 0.0)
    values_ref[...] = nt_dot(member, largest, HIGHEST)

    cands = jnp.concatenate([keep_ref[half:, :], from_side_ref[half:, :]], axis=0)
    entries = cands.shape[0]
    own = (pos & ~sum(outer)) | spread(iota((n_out, DIM), 0), outer)
    slots = chosen_ref.shape[1]
    slot = iota((entries, slots), 1)
    entry = iota((entries, slots), 0)
    same = at_steps(pos, [0, 1, side, side | 1], slot // CAP, entry)
    local = jnp.zeros((n_out, slots), jnp.float32)
    count = jnp.zeros((n_out, slots), jnp.float32)
    for c, at in enumerate(range(0, queries_n, DIM)):
        found = nt_dot(jnp.where(own - at == iota((n_out, DIM), 1), 1.0, 0.0), cands, HIGHEST)
        top = (CAP + 1) * c
        pick = jnp.where(same & (entry % 8 == top + slot % CAP), 1.0, 0.0)
        local += jnp.dot(found, pick, precision=HIGHEST, preferred_element_type=jnp.float32)
        pick = jnp.where(same & (entry % 8 == top + CAP), 1.0, 0.0)
        count += jnp.dot(found, pick, precision=HIGHEST, preferred_element_type=jnp.float32)
    live = (iota((n_out, slots), 1) % CAP).astype(jnp.float32) < count
    for p in range(held):
        chosen_ref[p * n_out:(p + 1) * n_out, :] = jnp.where(live & (local == float(p)), 1.0, 0.0)


def score_kernel(side, outer, held, n_tiles, pos_ref, *refs):
    wide_refs = refs[:n_tiles]
    values_ref, chosen_ref, mine_ref, theirs_ref, out_ref = refs[n_tiles:]
    pos = pos_ref[0]
    n_out = 1 << len(outer)
    half = n_out * EXP
    sums = mine_ref[...] + theirs_ref[...]
    scale = lax.rsqrt(jnp.mean(sums * sums, axis=1, keepdims=True) + 1e-05)
    order = (iota((half, 1), 0) % EXP).astype(jnp.float32)
    extra = sums * (scale * (BETA * jnp.log((NCENT + 1.0) / (order + 1.0))))
    if half % DIM > 0:
        extra = jnp.concatenate([extra, jnp.zeros((-half % DIM, DIM), jnp.float32)], axis=0)
    parts = [[] for _ in wide_refs]
    for at in range(0, half, DIM):
        high, low = split(extra[at:at + DIM])
        right = jnp.concatenate([
            jnp.concatenate([high, high], axis=1),
            jnp.concatenate([low, jnp.zeros_like(low)], axis=1),
        ], axis=0)
        for i, wide in enumerate(wide_refs):
            both = nt_dot(wide[...], right)
            parts[i].append(over_tokens(both[:, :DIM] + both[:, DIM:]))
    largest = largest_rows([jnp.concatenate(part, axis=1) for part in parts], held)
    total = largest.shape[1]
    col = iota((n_out, 3 * total), 1) % total
    member = jnp.where(col // EXP == iota((n_out, 3 * total), 0), 1.0 / QL, 0.0).astype(jnp.bfloat16)
    values = values_ref[...] + nt_dot(member, jnp.concatenate(thirds(largest), axis=1))
    slots = out_ref.shape[1]
    padded = slots + (-slots % DIM)
    shape = (n_tiles * 8, held * padded)
    entry = iota(shape, 0)
    col = iota(shape, 1)
    same = at_steps(pos, [0, side, 1, side | 1], col % padded // CAP, entry) & (col % padded < slots)
    pick = jnp.where(same & (entry % 8 == col // padded), 1.0, 0.0).astype(jnp.bfloat16)
    found = jnp.dot(jnp.concatenate(thirds(values), axis=0), pick, preferred_element_type=jnp.float32)
    found = found[:n_out] + found[n_out:2 * n_out] + found[2 * n_out:]
    result = jnp.zeros((n_out, slots), jnp.float32)
    for p in range(held):
        value = found[:, p * padded:p * padded + slots]
        result = jnp.where(chosen_ref[p * n_out:(p + 1) * n_out, :] > 0.5, value, result)
    out_ref[...] = result


def call(kernel, outs, *args, copied=False):
    smem = pl.BlockSpec(memory_space=pltpu.SMEM)
    vmem = pl.BlockSpec(memory_space=pltpu.VMEM)
    specs = [smem if a.ndim == 1 else vmem for a in args]
    scratch = []
    if copied:
        specs[1:] = [pl.BlockSpec(memory_space=pltpu.HBM)] * (len(args) - 1)
        scratch = [(pltpu.SMEM if a.ndim == 1 else pltpu.VMEM)(a.shape, a.dtype) for a in args[1:]]
        scratch += [pltpu.SemaphoreType.DMA((len(args) - 1,))]
        args = args[:1] + tuple(pltpu.with_memory_space_constraint(a, pltpu.HBM) for a in args[1:])
    return pl.pallas_call(
        kernel,
        out_shape=[pltpu.VMEM(o.shape, o.dtype) for o in outs] if len(outs) > 1 else outs[0],
        in_specs=specs,
        out_specs=[vmem] * len(outs) if len(outs) > 1 else vmem,
        scratch_shapes=scratch,
        compiler_params=pltpu.CompilerParams(vmem_limit_bytes=24 * 1024 * 1024),
    )(*args)


def body(queries, passages, clusters, lengths, feedback, ranks, cand_local, cand_count):
    held, tokens, _ = passages.shape
    queries_n = feedback.shape[0]
    n_corpus = lax.axis_size("corpus")
    devices = lax.axis_size("query") * n_corpus
    side, last = n_corpus, 2 * n_corpus
    masks = [1 << k for k in range(devices.bit_length() - 1)]
    outer = [m for m in reversed(masks) if 1 < m < n_corpus] + [m for m in masks if m >= last]
    asking = outer[1:] + outer[:1]
    n_out = 1 << len(outer)
    pos = lax.axis_index(AXES).astype(jnp.int32).reshape(1)

    def swap(x, mask):
        return lax.ppermute(x, AXES, [(i, i ^ mask) for i in range(devices)])

    def struct(rows, cols=DIM):
        return jax.ShapeDtypeStruct((rows, cols), jnp.float32)

    chunks = -(-queries_n // DIM)
    pay_rows = ASK_ROW
    assert (CAP + 1) * chunks <= 8 and queries.shape[0] == 1 and 8 % held == 0
    tiles = jnp.transpose(passages, (1, 0, 2)).reshape(tokens * held, DIM)
    masked, pay = call(
        functools.partial(pairs_kernel, queries_n, held, tokens),
        [struct(tokens * held), struct(pay_rows)],
        pos, lengths, tiles, clusters, feedback.T, ranks.T, cand_local.T, cand_count.T, copied=True,
    )
    def together(*xs):
        return lax.optimization_barrier(xs)

    def joined(xs):
        return xs[0] if len(xs) == 1 else jnp.concatenate(xs, axis=0)

    beside = swap(pay, 1)
    half = n_out * EXP
    keep, send = call(functools.partial(combine_kernel, side, outer), [struct(half + 16)] * 2, pos, pay, beside)
    from_side = swap(send, side)
    sums = keep[:half] + from_side[:half]
    asks = [queries[0]]
    for mask in asking:
        asks = asks + [swap(joined(asks), mask)]
    masked, _ = lax.optimization_barrier((masked, asks[1]))
    far = swap(masked, side)
    for mask in outer[:-1]:
        sums = sums + swap(sums, mask)
    far, sums, asks = lax.optimization_barrier((far, sums, asks))
    came = swap(sums, outer[-1])
    tiles = [masked, far]
    tiles = tiles + [swap(t, 1) for t in tiles]
    slots = devices * CAP
    wide = jax.ShapeDtypeStruct((tokens * held, 2 * DIM), jnp.bfloat16)
    *tiles, values, chosen = call(
        functools.partial(match_kernel, side, outer, asking, queries_n, held, len(tiles), len(asks)),
        [wide] * len(tiles) + [struct(n_out, 8 * len(tiles)), struct(held * n_out, slots)],
        pos, *tiles, *asks, keep, from_side,
    )
    table = call(
        functools.partial(score_kernel, side, outer, held, len(tiles)), [struct(n_out, slots)],
        pos, *tiles, values, chosen, sums, came,
    )
    for mask in reversed(outer):
        table = table + swap(table, mask)
    mine = sum(jnp.where((pos[0] & mask) != 0, 1 << k, 0) for k, mask in enumerate(outer))
    return lax.dynamic_slice(table, (mine, 0), (1, devices * CAP))


def solution(mesh):
    in_specs = (
        P(AXES, None, None),
        P(AXES, None, None),
        P(AXES, None),
        P(AXES),
        P(),
        P(),
        P(None, AXES),
        P(None, AXES),
    )
    return jax.shard_map(body, mesh=mesh, in_specs=in_specs, out_specs=P(AXES, None), check_vma=False)
```

```python
import functools

import jax
import jax.numpy as jnp
from jax import lax
from jax.experimental import pallas as pl
from jax.experimental.pallas import tpu as pltpu
from jax.sharding import PartitionSpec as P

DIM = 128
QL = 32
NCENT = 24
EXP = 10
CAP = 2
FB = 3
BETA = 0.5
AXES = ("query", "corpus")
ID_ROW = 31
CAND_ROW = 32
ASK_ROW = 40
HIGHEST = lax.Precision.HIGHEST


def iota(shape, axis):
    return lax.broadcasted_iota(jnp.int32, shape, axis)


def spread(index, masks):
    total = 0
    for k, mask in enumerate(masks):
        total = total | (((index >> k) & 1) * mask)
    return total


def gather_bits(device, masks):
    total = 0
    for k, mask in enumerate(masks):
        total = total | (jnp.where((device & mask) != 0, 1, 0) << k)
    return total


def pairs_kernel(queries_n, held, tokens, pos_ref, *refs):
    sources, (masked_ref, pay_ref) = refs[:7], refs[7:9]
    landed, sems = refs[9:16], refs[16]
    copies = [pltpu.make_async_copy(a, b, sems.at[k]) for k, (a, b) in enumerate(zip(sources, landed))]
    for copy in copies[::-1]:
        copy.start()
    for copy in copies[:1] + copies[2:]:
        copy.wait()
    len_ref, tiles_ref, clusters_ref, feedback_ref, ranks_ref, local_ref, count_ref = landed
    pos = pos_ref[0]
    nearby = feedback_ref[...] - pos * held
    number = (iota(nearby.shape, 0) * queries_n + iota(nearby.shape, 1)) * held + nearby
    here = (nearby >= 0) & (nearby < held)
    key = jnp.where(here, number, 0).astype(jnp.float32)
    least = jnp.min(jnp.where(here, key, 1e9))
    most = jnp.max(key)
    keys = [least, jnp.sum(key) - least - most, most]
    ranks = ranks_ref[...].astype(jnp.float32)
    lane = iota(ranks.shape, 1)
    pay_ref[:ASK_ROW, :] = jnp.zeros((ASK_ROW, DIM), jnp.float32)
    ids = jnp.zeros((1, DIM), jnp.float32)
    slot = iota((1, DIM), 1) // EXP
    kinds = iota((NCENT, tokens), 0)
    times = iota((EXP, tokens), 1)
    wanted = iota((EXP, tokens), 0).astype(jnp.float32)
    pairs = []
    for s in range(FB):
        whole = keys[s].astype(jnp.int32)
        p = whole % held
        q = (whole // held) % queries_n
        ids = jnp.where(slot == s, q.astype(jnp.float32), ids)
        rank = jnp.sum(jnp.where(lane == q, ranks, 0.0), axis=1, keepdims=True)
        kind = clusters_ref[pl.ds(p, 1), :]
        of_token = jnp.sum(jnp.where(kind == kinds, rank, 0.0), axis=0, keepdims=True)
        pairs.append((p, jnp.where((of_token == wanted) & (times < len_ref[p]), 1.0, 0.0).astype(jnp.bfloat16)))
    copies[1].wait()
    for s, (p, chosen) in enumerate(pairs):
        passage = tiles_ref[pl.ds(p, tokens, stride=held), :]
        pieces = jnp.dot(chosen, jnp.concatenate(thirds(passage), axis=1), preferred_element_type=jnp.float32)
        pay_ref[s * EXP:(s + 1) * EXP, :] = pieces[:, 2 * DIM:] + pieces[:, DIM:2 * DIM] + pieces[:, :DIM]
    per_tile = 8 // held
    row = iota((8, DIM), 0)
    limit = jnp.zeros((8, DIM), jnp.int32)
    for p in range(held):
        limit = jnp.where(row % held == p, len_ref[p], limit)
    first = tiles_ref[0:held, :]
    first = jnp.concatenate([first] * per_tile, axis=0)
    groups = tokens * held // 8
    token = iota((groups, 8, DIM), 0) * per_tile + (iota((groups, 8, DIM), 1) // held)
    tiles = tiles_ref[...].reshape(groups, 8, DIM)
    masked_ref[...] = jnp.where(token < limit[None], tiles, first[None]).reshape(groups * 8, DIM)

    pay_ref[ID_ROW:ID_ROW + 1, :] = ids
    for c, at in enumerate(range(0, queries_n, DIM)):
        width = min(DIM, queries_n - at)
        top = CAND_ROW + (CAP + 1) * c
        pay_ref[top:top + CAP, 0:width] = local_ref[:, at:at + width].astype(jnp.float32)
        pay_ref[top + CAP:top + CAP + 1, 0:width] = count_ref[:, at:at + width].astype(jnp.float32)


def combine_kernel(side, outer, pos_ref, *refs):
    *pays, keep_ref, send_ref = refs
    pos = pos_ref[0]
    half = (1 << len(outer)) * EXP
    rows = 2 * half
    row = iota((rows, DIM), 0)
    owner = ((pos ^ ((row // half) * side)) & (1 | side)) | spread(row % half // EXP, outer)
    owner = owner.astype(jnp.float32)
    places = [(pay, 0) for pay in pays]
    total = jnp.zeros((rows, DIM), jnp.float32)
    for group in range(0, len(places), 8):
        some = places[group:group + 8]
        ids = jnp.concatenate([pay[at + ID_ROW:at + ID_ROW + 1, :CAND_ROW] for pay, at in some], axis=1)
        col = iota((rows, ids.shape[1]), 1) % CAND_ROW
        pick = (col % EXP == row[:, :1] % EXP) & (col < FB * EXP) & (ids == owner[:, :1])
        pick = jnp.where(pick, 1.0, 0.0).astype(jnp.bfloat16)
        block = jnp.concatenate([pay[at:at + CAND_ROW, :] for pay, at in some], axis=0)
        for piece in thirds(block)[::-1]:
            total += jnp.dot(pick, piece, preferred_element_type=jnp.float32)
    for ref, sums in ((keep_ref, total[:rows // 2]), (send_ref, total[rows // 2:])):
        ref[:rows // 2, :] = sums
        ref[rows // 2:rows // 2 + 8, :] = pays[0][CAND_ROW:ASK_ROW, :]
        ref[rows // 2 + 8:, :] = pays[-1][CAND_ROW:ASK_ROW, :]


def nt_dot(a, b, precision=None):
    return lax.dot_general(a, b, (((1,), (1,)), ((), ())), precision=precision, preferred_element_type=jnp.float32)


def thirds(x):
    high, low = split(x)
    return high, low, (x - high.astype(jnp.float32) - low.astype(jnp.float32)).astype(jnp.bfloat16)


def split(x):
    high = x.astype(jnp.bfloat16)
    return high, (x - high.astype(jnp.float32)).astype(jnp.bfloat16)


def at_steps(pos, steps, device, entry):
    place = jnp.zeros(entry.shape, jnp.int32)
    for i, away in enumerate(steps):
        place = jnp.where(entry // 8 == i, pos ^ away, place)
    return place == device


def largest_rows(parts, held):
    rows = []
    for top in parts:
        step = held
        while step < 8:
            top = jnp.maximum(top, pltpu.roll(top, step, 0))
            step *= 2
        rows.append(top)
    return jnp.concatenate(rows, axis=0)


def over_tokens(similar):
    return jnp.max(similar.reshape(similar.shape[0] // 8, 8, similar.shape[1]), axis=0)


def match_kernel(side, outer, asking, queries_n, held, n_tiles, n_asks, pos_ref, *refs):
    tile_refs, ask_refs = refs[:n_tiles], refs[n_tiles:n_tiles + n_asks]
    keep_ref, from_side_ref = refs[n_tiles + n_asks:n_tiles + n_asks + 2]
    *wide_refs, values_ref, chosen_ref = refs[n_tiles + n_asks + 2:]
    pos = pos_ref[0]
    n_out = 1 << len(outer)
    me_out = gather_bits(pos, outer)
    half = n_out * EXP
    tokens = jnp.concatenate([ask[...] for ask in ask_refs], axis=0)
    total = tokens.shape[0]
    lefts = []
    for ref, wide_ref in zip(tile_refs, wide_refs):
        high, low = split(ref[...])
        wide = jnp.concatenate([high, low], axis=1)
        wide_ref[...] = wide
        lefts.append((high, wide))
    parts = [[] for _ in lefts]
    for at in range(0, total, 256):
        high, low = split(tokens[at:at + 256])
        twice = jnp.concatenate([high, high], axis=1)
        for i, (left, wide) in enumerate(lefts):
            parts[i].append(over_tokens(nt_dot(wide, twice) + nt_dot(left, low)))
    largest = largest_rows([jnp.concatenate(part, axis=1) for part in parts], held)
    of_col = gather_bits(spread(iota((n_out, total), 1) // QL, asking), outer) ^ me_out
    member = jnp.where(of_col == iota((n_out, total), 0), 1.0 / QL, 0.0)
    values_ref[...] = nt_dot(member, largest, HIGHEST)

    cands = jnp.concatenate([keep_ref[half:, :], from_side_ref[half:, :]], axis=0)
    entries = cands.shape[0]
    own = (pos & ~sum(outer)) | spread(iota((n_out, DIM), 0), outer)
    slots = chosen_ref.shape[1]
    slot = iota((entries, slots), 1)
    entry = iota((entries, slots), 0)
    same = at_steps(pos, [0, 1, side, side | 1], slot // CAP, entry)
    local = jnp.zeros((n_out, slots), jnp.float32)
    count = jnp.zeros((n_out, slots), jnp.float32)
    for c, at in enumerate(range(0, queries_n, DIM)):
        found = nt_dot(jnp.where(own - at == iota((n_out, DIM), 1), 1.0, 0.0), cands, HIGHEST)
        top = (CAP + 1) * c
        pick = jnp.where(same & (entry % 8 == top + slot % CAP), 1.0, 0.0)
        local += jnp.dot(found, pick, precision=HIGHEST, preferred_element_type=jnp.float32)
        pick = jnp.where(same & (entry % 8 == top + CAP), 1.0, 0.0)
        count += jnp.dot(found, pick, precision=HIGHEST, preferred_element_type=jnp.float32)
    live = (iota((n_out, slots), 1) % CAP).astype(jnp.float32) < count
    for p in range(held):
        chosen_ref[p * n_out:(p + 1) * n_out, :] = jnp.where(live & (local == float(p)), 1.0, 0.0)


def score_kernel(side, outer, held, n_tiles, pos_ref, *refs):
    wide_refs = refs[:n_tiles]
    values_ref, chosen_ref, mine_ref, theirs_ref, out_ref = refs[n_tiles:]
    pos = pos_ref[0]
    n_out = 1 << len(outer)
    half = n_out * EXP
    sums = mine_ref[...] + theirs_ref[...]
    scale = lax.rsqrt(jnp.mean(sums * sums, axis=1, keepdims=True) + 1e-05)
    order = (iota((half, 1), 0) % EXP).astype(jnp.float32)
    extra = sums * (scale * (BETA * jnp.log((NCENT + 1.0) / (order + 1.0))))
    if half % DIM > 0:
        extra = jnp.concatenate([extra, jnp.zeros((-half % DIM, DIM), jnp.float32)], axis=0)
    parts = [[] for _ in wide_refs]
    for at in range(0, half, DIM):
        high, low = split(extra[at:at + DIM])
        right = jnp.concatenate([
            jnp.concatenate([high, high], axis=1),
            jnp.concatenate([low, jnp.zeros_like(low)], axis=1),
        ], axis=0)
        for i, wide in enumerate(wide_refs):
            both = nt_dot(wide[...], right)
            parts[i].append(over_tokens(both[:, :DIM] + both[:, DIM:]))
    largest = largest_rows([jnp.concatenate(part, axis=1) for part in parts], held)
    total = largest.shape[1]
    col = iota((n_out, 3 * total), 1) % total
    member = jnp.where(col // EXP == iota((n_out, 3 * total), 0), 1.0 / QL, 0.0).astype(jnp.bfloat16)
    values = values_ref[...] + nt_dot(member, jnp.concatenate(thirds(largest), axis=1))
    slots = out_ref.shape[1]
    padded = slots + (-slots % DIM)
    shape = (n_tiles * 8, held * padded)
    entry = iota(shape, 0)
    col = iota(shape, 1)
    same = at_steps(pos, [0, side, 1, side | 1], col % padded // CAP, entry) & (col % padded < slots)
    pick = jnp.where(same & (entry % 8 == col // padded), 1.0, 0.0).astype(jnp.bfloat16)
    found = jnp.dot(jnp.concatenate(thirds(values), axis=0), pick, preferred_element_type=jnp.float32)
    found = found[:n_out] + found[n_out:2 * n_out] + found[2 * n_out:]
    result = jnp.zeros((n_out, slots), jnp.float32)
    for p in range(held):
        value = found[:, p * padded:p * padded + slots]
        result = jnp.where(chosen_ref[p * n_out:(p + 1) * n_out, :] > 0.5, value, result)
    out_ref[...] = result


def call(kernel, outs, *args, copied=False):
    smem = pl.BlockSpec(memory_space=pltpu.SMEM)
    vmem = pl.BlockSpec(memory_space=pltpu.VMEM)
    specs = [smem if a.ndim == 1 else vmem for a in args]
    scratch = []
    if copied:
        specs[1:] = [pl.BlockSpec(memory_space=pltpu.HBM)] * (len(args) - 1)
        scratch = [(pltpu.SMEM if a.ndim == 1 else pltpu.VMEM)(a.shape, a.dtype) for a in args[1:]]
        scratch += [pltpu.SemaphoreType.DMA((len(args) - 1,))]
        args = args[:1] + tuple(pltpu.with_memory_space_constraint(a, pltpu.HBM) for a in args[1:])
    return pl.pallas_call(
        kernel,
        out_shape=[pltpu.VMEM(o.shape, o.dtype) for o in outs] if len(outs) > 1 else outs[0],
        in_specs=specs,
        out_specs=[vmem] * len(outs) if len(outs) > 1 else vmem,
        scratch_shapes=scratch,
        compiler_params=pltpu.CompilerParams(vmem_limit_bytes=24 * 1024 * 1024),
    )(*args)


def body(queries, passages, clusters, lengths, feedback, ranks, cand_local, cand_count):
    held, tokens, _ = passages.shape
    queries_n = feedback.shape[0]
    n_corpus = lax.axis_size("corpus")
    devices = lax.axis_size("query") * n_corpus
    side, last = n_corpus, 2 * n_corpus
    masks = [1 << k for k in range(devices.bit_length() - 1)]
    outer = [m for m in reversed(masks) if 1 < m < n_corpus] + [m for m in masks if m >= last]
    asking = outer[1:] + outer[:1]
    n_out = 1 << len(outer)
    pos = lax.axis_index(AXES).astype(jnp.int32).reshape(1)

    def swap(x, mask):
        return lax.ppermute(x, AXES, [(i, i ^ mask) for i in range(devices)])

    def struct(rows, cols=DIM):
        return jax.ShapeDtypeStruct((rows, cols), jnp.float32)

    chunks = -(-queries_n // DIM)
    pay_rows = ASK_ROW
    assert (CAP + 1) * chunks <= 8 and queries.shape[0] == 1 and 8 % held == 0
    tiles = jnp.transpose(passages, (1, 0, 2)).reshape(tokens * held, DIM)
    masked, pay = call(
        functools.partial(pairs_kernel, queries_n, held, tokens),
        [struct(tokens * held), struct(pay_rows)],
        pos, lengths, tiles, clusters, feedback.T, ranks.T, cand_local.T, cand_count.T, copied=True,
    )
    def together(*xs):
        return lax.optimization_barrier(xs)

    def joined(xs):
        return xs[0] if len(xs) == 1 else jnp.concatenate(xs, axis=0)

    beside = swap(pay, 1)
    half = n_out * EXP
    keep, send = call(functools.partial(combine_kernel, side, outer), [struct(half + 16)] * 2, pos, pay, beside)
    from_side = swap(send, side)
    sums = keep[:half] + from_side[:half]
    asks = [queries[0]]
    for mask in asking:
        asks = asks + [swap(joined(asks), mask)]
    masked, _ = lax.optimization_barrier((masked, asks[1]))
    far = swap(masked, side)
    for mask in outer[:-1]:
        sums = sums + swap(sums, mask)
    far, sums, asks = lax.optimization_barrier((far, sums, asks))
    came = swap(sums, outer[-1])
    tiles = [masked, far]
    tiles = tiles + [swap(t, 1) for t in tiles]
    slots = devices * CAP
    wide = jax.ShapeDtypeStruct((tokens * held, 2 * DIM), jnp.bfloat16)
    *tiles, values, chosen = call(
        functools.partial(match_kernel, side, outer, asking, queries_n, held, len(tiles), len(asks)),
        [wide] * len(tiles) + [struct(n_out, 8 * len(tiles)), struct(held * n_out, slots)],
        pos, *tiles, *asks, keep, from_side,
    )
    table = call(
        functools.partial(score_kernel, side, outer, held, len(tiles)), [struct(n_out, slots)],
        pos, *tiles, values, chosen, sums, came,
    )
    for mask in reversed(outer):
        table = table + swap(table, mask)
    mine = sum(jnp.where((pos[0] & mask) != 0, 1 << k, 0) for k, mask in enumerate(outer))
    return lax.dynamic_slice(table, (mine, 0), (1, devices * CAP))


def solution(mesh):
    in_specs = (
        P(AXES, None, None),
        P(AXES, None, None),
        P(AXES, None),
        P(AXES),
        P(),
        P(),
        P(None, AXES),
        P(None, AXES),
    )
    return jax.shard_map(body, mesh=mesh, in_specs=in_specs, out_specs=P(AXES, None), check_vma=False)
```

```python
import functools

import jax
import jax.numpy as jnp
from jax import lax
from jax.experimental import pallas as pl
from jax.experimental.pallas import tpu as pltpu
from jax.sharding import PartitionSpec as P

DIM = 128
QL = 32
NCENT = 24
EXP = 10
CAP = 2
FB = 3
BETA = 0.5
AXES = ("query", "corpus")
ID_ROW = 31
CAND_ROW = 32
ASK_ROW = 40
HIGHEST = lax.Precision.HIGHEST


def iota(shape, axis):
    return lax.broadcasted_iota(jnp.int32, shape, axis)


def spread(index, steps):
    total = 0
    for k, step in enumerate(steps):
        total = total ^ (((index >> k) & 1) * step)
    return total


def gather_bits(device, bits):
    total = 0
    for k, bit in enumerate(bits):
        total = total | (jnp.where((device & bit) != 0, 1, 0) << k)
    return total


def steps_of(bits):
    return [bit | 1 for bit in bits]


def owner_of(pos, index, bits):
    return pos ^ spread(gather_bits(pos, bits) ^ index, steps_of(bits))


def pairs_kernel(queries_n, held, tokens, pos_ref, *refs):
    sources, (masked_ref, pay_ref) = refs[:7], refs[7:9]
    landed, sems = refs[9:16], refs[16]
    copies = [pltpu.make_async_copy(a, b, sems.at[k]) for k, (a, b) in enumerate(zip(sources, landed))]
    for copy in copies[::-1]:
        copy.start()
    for copy in copies[:1] + copies[2:]:
        copy.wait()
    len_ref, tiles_ref, clusters_ref, feedback_ref, ranks_ref, local_ref, count_ref = landed
    pos = pos_ref[0]
    nearby = feedback_ref[...] - pos * held
    number = (iota(nearby.shape, 0) * queries_n + iota(nearby.shape, 1)) * held + nearby
    here = (nearby >= 0) & (nearby < held)
    key = jnp.where(here, number, 0).astype(jnp.float32)
    least = jnp.min(jnp.where(here, key, 1e9))
    most = jnp.max(key)
    keys = [least, jnp.sum(key) - least - most, most]
    ranks = ranks_ref[...].astype(jnp.float32)
    lane = iota(ranks.shape, 1)
    pay_ref[:ASK_ROW, :] = jnp.zeros((ASK_ROW, DIM), jnp.float32)
    ids = jnp.zeros((1, DIM), jnp.float32)
    slot = iota((1, DIM), 1) // EXP
    kinds = iota((NCENT, tokens), 0)
    times = iota((EXP, tokens), 1)
    wanted = iota((EXP, tokens), 0).astype(jnp.float32)
    pairs = []
    for s in range(FB):
        whole = keys[s].astype(jnp.int32)
        p = whole % held
        q = (whole // held) % queries_n
        ids = jnp.where(slot == s, q.astype(jnp.float32), ids)
        rank = jnp.sum(jnp.where(lane == q, ranks, 0.0), axis=1, keepdims=True)
        kind = clusters_ref[pl.ds(p, 1), :]
        of_token = jnp.sum(jnp.where(kind == kinds, rank, 0.0), axis=0, keepdims=True)
        pairs.append((p, jnp.where((of_token == wanted) & (times < len_ref[p]), 1.0, 0.0).astype(jnp.bfloat16)))
    copies[1].wait()
    for s, (p, chosen) in enumerate(pairs):
        passage = tiles_ref[pl.ds(p, tokens, stride=held), :]
        pieces = jnp.dot(chosen, jnp.concatenate(thirds(passage), axis=1), preferred_element_type=jnp.float32)
        pay_ref[s * EXP:(s + 1) * EXP, :] = pieces[:, 2 * DIM:] + pieces[:, DIM:2 * DIM] + pieces[:, :DIM]
    per_tile = 8 // held
    row = iota((8, DIM), 0)
    limit = jnp.zeros((8, DIM), jnp.int32)
    for p in range(held):
        limit = jnp.where(row % held == p, len_ref[p], limit)
    first = tiles_ref[0:held, :]
    first = jnp.concatenate([first] * per_tile, axis=0)
    groups = tokens * held // 8
    token = iota((groups, 8, DIM), 0) * per_tile + (iota((groups, 8, DIM), 1) // held)
    tiles = tiles_ref[...].reshape(groups, 8, DIM)
    masked_ref[...] = jnp.where(token < limit[None], tiles, first[None]).reshape(groups * 8, DIM)

    pay_ref[ID_ROW:ID_ROW + 1, :] = ids
    for c, at in enumerate(range(0, queries_n, DIM)):
        width = min(DIM, queries_n - at)
        top = CAND_ROW + (CAP + 1) * c
        pay_ref[top:top + CAP, 0:width] = local_ref[:, at:at + width].astype(jnp.float32)
        pay_ref[top + CAP:top + CAP + 1, 0:width] = count_ref[:, at:at + width].astype(jnp.float32)


def combine_kernel(side, outer, pos_ref, *refs):
    *pays, keep_ref, send_ref = refs
    pos = pos_ref[0]
    half = (1 << len(outer)) * EXP
    rows = 2 * half
    row = iota((rows, DIM), 0)
    owner = owner_of(pos, row % half // EXP, outer) ^ ((row // half) * side)
    owner = owner.astype(jnp.float32)
    places = [(pay, 0) for pay in pays]
    total = jnp.zeros((rows, DIM), jnp.float32)
    for group in range(0, len(places), 8):
        some = places[group:group + 8]
        ids = jnp.concatenate([pay[at + ID_ROW:at + ID_ROW + 1, :CAND_ROW] for pay, at in some], axis=1)
        col = iota((rows, ids.shape[1]), 1) % CAND_ROW
        pick = (col % EXP == row[:, :1] % EXP) & (col < FB * EXP) & (ids == owner[:, :1])
        pick = jnp.where(pick, 1.0, 0.0).astype(jnp.bfloat16)
        block = jnp.concatenate([pay[at:at + CAND_ROW, :] for pay, at in some], axis=0)
        for piece in thirds(block)[::-1]:
            total += jnp.dot(pick, piece, preferred_element_type=jnp.float32)
    for ref, sums in ((keep_ref, total[:rows // 2]), (send_ref, total[rows // 2:])):
        ref[:rows // 2, :] = sums
        ref[rows // 2:rows // 2 + 8, :] = pays[0][CAND_ROW:ASK_ROW, :]
        ref[rows // 2 + 8:, :] = pays[-1][CAND_ROW:ASK_ROW, :]


def nt_dot(a, b, precision=None):
    return lax.dot_general(a, b, (((1,), (1,)), ((), ())), precision=precision, preferred_element_type=jnp.float32)


def thirds(x):
    high, low = split(x)
    return high, low, (x - high.astype(jnp.float32) - low.astype(jnp.float32)).astype(jnp.bfloat16)


def split(x):
    high = x.astype(jnp.bfloat16)
    return high, (x - high.astype(jnp.float32)).astype(jnp.bfloat16)


def at_steps(pos, steps, device, entry):
    place = jnp.zeros(entry.shape, jnp.int32)
    for i, away in enumerate(steps):
        place = jnp.where(entry // 8 == i, pos ^ away, place)
    return place == device


def largest_rows(parts, held):
    rows = []
    for top in parts:
        step = held
        while step < 8:
            top = jnp.maximum(top, pltpu.roll(top, step, 0))
            step *= 2
        rows.append(top)
    return jnp.concatenate(rows, axis=0)


def over_tokens(similar):
    return jnp.max(similar.reshape(similar.shape[0] // 8, 8, similar.shape[1]), axis=0)


def match_kernel(side, outer, asking, queries_n, held, n_tiles, n_asks, pos_ref, *refs):
    tile_refs, ask_refs = refs[:n_tiles], refs[n_tiles:n_tiles + n_asks]
    keep_ref, from_side_ref = refs[n_tiles + n_asks:n_tiles + n_asks + 2]
    *wide_refs, values_ref, chosen_ref = refs[n_tiles + n_asks + 2:]
    pos = pos_ref[0]
    n_out = 1 << len(outer)
    me_out = gather_bits(pos, outer)
    half = n_out * EXP
    tokens = jnp.concatenate([ask[...] for ask in ask_refs], axis=0)
    total = tokens.shape[0]
    lefts = []
    for ref, wide_ref in zip(tile_refs, wide_refs):
        high, low = split(ref[...])
        wide = jnp.concatenate([high, low], axis=1)
        wide_ref[...] = wide
        lefts.append((high, wide))
    parts = [[] for _ in lefts]
    for at in range(0, total, 256):
        high, low = split(tokens[at:at + 256])
        twice = jnp.concatenate([high, high], axis=1)
        for i, (left, wide) in enumerate(lefts):
            parts[i].append(over_tokens(nt_dot(wide, twice) + nt_dot(left, low)))
    largest = largest_rows([jnp.concatenate(part, axis=1) for part in parts], held)
    of_col = gather_bits(spread(iota((n_out, total), 1) // QL, steps_of(asking)), outer) ^ me_out
    member = jnp.where(of_col == iota((n_out, total), 0), 1.0 / QL, 0.0)
    values_ref[...] = nt_dot(member, largest, HIGHEST)

    cands = jnp.concatenate([keep_ref[half:, :], from_side_ref[half:, :]], axis=0)
    entries = cands.shape[0]
    own = owner_of(pos, iota((n_out, DIM), 0), outer)
    slots = chosen_ref.shape[1]
    slot = iota((entries, slots), 1)
    entry = iota((entries, slots), 0)
    same = at_steps(pos, [0, 1, side, side ^ 1], slot // CAP, entry)
    local = jnp.zeros((n_out, slots), jnp.float32)
    count = jnp.zeros((n_out, slots), jnp.float32)
    for c, at in enumerate(range(0, queries_n, DIM)):
        found = nt_dot(jnp.where(own - at == iota((n_out, DIM), 1), 1.0, 0.0), cands, HIGHEST)
        top = (CAP + 1) * c
        pick = jnp.where(same & (entry % 8 == top + slot % CAP), 1.0, 0.0)
        local += jnp.dot(found, pick, precision=HIGHEST, preferred_element_type=jnp.float32)
        pick = jnp.where(same & (entry % 8 == top + CAP), 1.0, 0.0)
        count += jnp.dot(found, pick, precision=HIGHEST, preferred_element_type=jnp.float32)
    live = (iota((n_out, slots), 1) % CAP).astype(jnp.float32) < count
    for p in range(held):
        chosen_ref[p * n_out:(p + 1) * n_out, :] = jnp.where(live & (local == float(p)), 1.0, 0.0)


def score_kernel(side, outer, held, n_tiles, pos_ref, *refs):
    wide_refs = refs[:n_tiles]
    values_ref, chosen_ref, mine_ref, theirs_ref, out_ref = refs[n_tiles:]
    pos = pos_ref[0]
    n_out = 1 << len(outer)
    half = n_out * EXP
    sums = mine_ref[...] + theirs_ref[...]
    scale = lax.rsqrt(jnp.mean(sums * sums, axis=1, keepdims=True) + 1e-05)
    order = (iota((half, 1), 0) % EXP).astype(jnp.float32)
    extra = sums * (scale * (BETA * jnp.log((NCENT + 1.0) / (order + 1.0))))
    if half % DIM > 0:
        extra = jnp.concatenate([extra, jnp.zeros((-half % DIM, DIM), jnp.float32)], axis=0)
    parts = [[] for _ in wide_refs]
    for at in range(0, half, DIM):
        high, low = split(extra[at:at + DIM])
        right = jnp.concatenate([
            jnp.concatenate([high, high], axis=1),
            jnp.concatenate([low, jnp.zeros_like(low)], axis=1),
        ], axis=0)
        for i, wide in enumerate(wide_refs):
            both = nt_dot(wide[...], right)
            parts[i].append(over_tokens(both[:, :DIM] + both[:, DIM:]))
    largest = largest_rows([jnp.concatenate(part, axis=1) for part in parts], held)
    total = largest.shape[1]
    col = iota((n_out, 3 * total), 1) % total
    member = jnp.where(col // EXP == iota((n_out, 3 * total), 0), 1.0 / QL, 0.0).astype(jnp.bfloat16)
    values = values_ref[...] + nt_dot(member, jnp.concatenate(thirds(largest), axis=1))
    slots = out_ref.shape[1]
    padded = slots + (-slots % DIM)
    shape = (n_tiles * 8, held * padded)
    entry = iota(shape, 0)
    col = iota(shape, 1)
    same = at_steps(pos, [0, side, 1, side ^ 1], col % padded // CAP, entry) & (col % padded < slots)
    pick = jnp.where(same & (entry % 8 == col // padded), 1.0, 0.0).astype(jnp.bfloat16)
    found = jnp.dot(jnp.concatenate(thirds(values), axis=0), pick, preferred_element_type=jnp.float32)
    found = found[:n_out] + found[n_out:2 * n_out] + found[2 * n_out:]
    result = jnp.zeros((n_out, slots), jnp.float32)
    for p in range(held):
        value = found[:, p * padded:p * padded + slots]
        result = jnp.where(chosen_ref[p * n_out:(p + 1) * n_out, :] > 0.5, value, result)
    out_ref[...] = result


def call(kernel, outs, *args, copied=False):
    smem = pl.BlockSpec(memory_space=pltpu.SMEM)
    vmem = pl.BlockSpec(memory_space=pltpu.VMEM)
    specs = [smem if a.ndim == 1 else vmem for a in args]
    scratch = []
    if copied:
        specs[1:] = [pl.BlockSpec(memory_space=pltpu.HBM)] * (len(args) - 1)
        scratch = [(pltpu.SMEM if a.ndim == 1 else pltpu.VMEM)(a.shape, a.dtype) for a in args[1:]]
        scratch += [pltpu.SemaphoreType.DMA((len(args) - 1,))]
        args = args[:1] + tuple(pltpu.with_memory_space_constraint(a, pltpu.HBM) for a in args[1:])
    return pl.pallas_call(
        kernel,
        out_shape=[pltpu.VMEM(o.shape, o.dtype) for o in outs] if len(outs) > 1 else outs[0],
        in_specs=specs,
        out_specs=[vmem] * len(outs) if len(outs) > 1 else vmem,
        scratch_shapes=scratch,
        compiler_params=pltpu.CompilerParams(vmem_limit_bytes=24 * 1024 * 1024),
    )(*args)


def body(queries, passages, clusters, lengths, feedback, ranks, cand_local, cand_count):
    held, tokens, _ = passages.shape
    queries_n = feedback.shape[0]
    n_corpus = lax.axis_size("corpus")
    devices = lax.axis_size("query") * n_corpus
    side, last = n_corpus | 1, 2 * n_corpus
    masks = [1 << k for k in range(devices.bit_length() - 1)]
    outer = [m for m in reversed(masks) if 1 < m < n_corpus] + [m for m in masks if m >= last]
    asking = outer[1:] + outer[:1]
    n_out = 1 << len(outer)
    pos = lax.axis_index(AXES).astype(jnp.int32).reshape(1)

    def swap(x, mask):
        return lax.ppermute(x, AXES, [(i, i ^ mask) for i in range(devices)])

    def struct(rows, cols=DIM):
        return jax.ShapeDtypeStruct((rows, cols), jnp.float32)

    chunks = -(-queries_n // DIM)
    pay_rows = ASK_ROW
    assert (CAP + 1) * chunks <= 8 and queries.shape[0] == 1 and 8 % held == 0
    tiles = jnp.transpose(passages, (1, 0, 2)).reshape(tokens * held, DIM)
    masked, pay = call(
        functools.partial(pairs_kernel, queries_n, held, tokens),
        [struct(tokens * held), struct(pay_rows)],
        pos, lengths, tiles, clusters, feedback.T, ranks.T, cand_local.T, cand_count.T, copied=True,
    )
    def together(*xs):
        return lax.optimization_barrier(xs)

    def joined(xs):
        return xs[0] if len(xs) == 1 else jnp.concatenate(xs, axis=0)

    beside = swap(pay, 1)
    half = n_out * EXP
    keep, send = call(functools.partial(combine_kernel, side, outer), [struct(half + 16)] * 2, pos, pay, beside)
    from_side = swap(send, side)
    sums = keep[:half] + from_side[:half]
    asks = [queries[0]]
    for step in steps_of(asking):
        asks = asks + [swap(joined(asks), step)]
    masked, _ = lax.optimization_barrier((masked, asks[1]))
    far = swap(masked, side)
    steps = steps_of(outer)
    for step in steps[:-1]:
        sums = sums + swap(sums, step)
    far, sums, asks = lax.optimization_barrier((far, sums, asks))
    came = swap(sums, steps[-1])
    tiles = [masked, far]
    tiles = tiles + [swap(t, 1) for t in tiles]
    slots = devices * CAP
    wide = jax.ShapeDtypeStruct((tokens * held, 2 * DIM), jnp.bfloat16)
    *tiles, values, chosen = call(
        functools.partial(match_kernel, side, outer, asking, queries_n, held, len(tiles), len(asks)),
        [wide] * len(tiles) + [struct(n_out, 8 * len(tiles)), struct(held * n_out, slots)],
        pos, *tiles, *asks, keep, from_side,
    )
    table = call(
        functools.partial(score_kernel, side, outer, held, len(tiles)), [struct(n_out, slots)],
        pos, *tiles, values, chosen, sums, came,
    )
    for step in reversed(steps):
        table = table + swap(table, step)
    return lax.dynamic_slice(table, (gather_bits(pos[0], outer), 0), (1, slots))


def solution(mesh):
    in_specs = (
        P(AXES, None, None),
        P(AXES, None, None),
        P(AXES, None),
        P(AXES),
        P(),
        P(),
        P(None, AXES),
        P(None, AXES),
    )
    return jax.shard_map(body, mesh=mesh, in_specs=in_specs, out_specs=P(AXES, None), check_vma=False)
```

```python
import functools

import jax
import jax.numpy as jnp
from jax import lax
from jax.experimental import pallas as pl
from jax.experimental.pallas import tpu as pltpu
from jax.sharding import PartitionSpec as P

DIM = 128
QL = 32
NCENT = 24
EXP = 10
CAP = 2
FB = 3
BETA = 0.5
AXES = ("query", "corpus")
ID_ROW = 31
CAND_ROW = 32
ASK_ROW = 40
HIGHEST = lax.Precision.HIGHEST


def iota(shape, axis):
    return lax.broadcasted_iota(jnp.int32, shape, axis)


def spread(index, steps):
    total = 0
    for k, step in enumerate(steps):
        total = total ^ (((index >> k) & 1) * step)
    return total


def gather_bits(device, bits):
    total = 0
    for k, bit in enumerate(bits):
        total = total | (jnp.where((device & bit) != 0, 1, 0) << k)
    return total


def steps_of(bits):
    return [bit | 1 for bit in bits]


def owner_of(pos, index, bits):
    return pos ^ spread(gather_bits(pos, bits) ^ index, steps_of(bits))


def pairs_kernel(queries_n, held, tokens, pos_ref, *refs):
    sources, (masked_ref, pay_ref) = refs[:7], refs[7:9]
    landed, sems = refs[9:16], refs[16]
    copies = [pltpu.make_async_copy(a, b, sems.at[k]) for k, (a, b) in enumerate(zip(sources, landed))]
    for copy in copies[::-1]:
        copy.start()
    for copy in copies[:1] + copies[2:]:
        copy.wait()
    len_ref, tiles_ref, clusters_ref, feedback_ref, ranks_ref, local_ref, count_ref = landed
    pos = pos_ref[0]
    nearby = feedback_ref[...] - pos * held
    number = (iota(nearby.shape, 0) * queries_n + iota(nearby.shape, 1)) * held + nearby
    here = (nearby >= 0) & (nearby < held)
    key = jnp.where(here, number, 0).astype(jnp.float32)
    least = jnp.min(jnp.where(here, key, 1e9))
    most = jnp.max(key)
    keys = [least, jnp.sum(key) - least - most, most]
    ranks = ranks_ref[...].astype(jnp.float32)
    lane = iota(ranks.shape, 1)
    pay_ref[:ASK_ROW, :] = jnp.zeros((ASK_ROW, DIM), jnp.float32)
    ids = jnp.zeros((1, DIM), jnp.float32)
    slot = iota((1, DIM), 1) // EXP
    kinds = iota((NCENT, tokens), 0)
    times = iota((EXP, tokens), 1)
    wanted = iota((EXP, tokens), 0).astype(jnp.float32)
    pairs = []
    for s in range(FB):
        whole = keys[s].astype(jnp.int32)
        p = whole % held
        q = (whole // held) % queries_n
        ids = jnp.where(slot == s, q.astype(jnp.float32), ids)
        rank = jnp.sum(jnp.where(lane == q, ranks, 0.0), axis=1, keepdims=True)
        kind = clusters_ref[pl.ds(p, 1), :]
        of_token = jnp.sum(jnp.where(kind == kinds, rank, 0.0), axis=0, keepdims=True)
        pairs.append((p, jnp.where((of_token == wanted) & (times < len_ref[p]), 1.0, 0.0).astype(jnp.bfloat16)))
    copies[1].wait()
    for s, (p, chosen) in enumerate(pairs):
        passage = tiles_ref[pl.ds(p, tokens, stride=held), :]
        pieces = jnp.dot(chosen, jnp.concatenate(thirds(passage), axis=1), preferred_element_type=jnp.float32)
        pay_ref[s * EXP:(s + 1) * EXP, :] = pieces[:, 2 * DIM:] + pieces[:, DIM:2 * DIM] + pieces[:, :DIM]
    per_tile = 8 // held
    row = iota((8, DIM), 0)
    limit = jnp.zeros((8, DIM), jnp.int32)
    for p in range(held):
        limit = jnp.where(row % held == p, len_ref[p], limit)
    first = tiles_ref[0:held, :]
    first = jnp.concatenate([first] * per_tile, axis=0)
    groups = tokens * held // 8
    token = iota((groups, 8, DIM), 0) * per_tile + (iota((groups, 8, DIM), 1) // held)
    tiles = tiles_ref[...].reshape(groups, 8, DIM)
    masked_ref[...] = jnp.where(token < limit[None], tiles, first[None]).reshape(groups * 8, DIM)

    pay_ref[ID_ROW:ID_ROW + 1, :] = ids
    for c, at in enumerate(range(0, queries_n, DIM)):
        width = min(DIM, queries_n - at)
        top = CAND_ROW + (CAP + 1) * c
        pay_ref[top:top + CAP, 0:width] = local_ref[:, at:at + width].astype(jnp.float32)
        pay_ref[top + CAP:top + CAP + 1, 0:width] = count_ref[:, at:at + width].astype(jnp.float32)


def combine_kernel(side, outer, pos_ref, *refs):
    *pays, keep_ref, send_ref = refs
    pos = pos_ref[0]
    half = (1 << len(outer)) * EXP
    rows = 2 * half
    row = iota((rows, DIM), 0)
    owner = owner_of(pos, row % half // EXP, outer) ^ ((row // half) * side)
    owner = owner.astype(jnp.float32)
    places = [(pay, 0) for pay in pays]
    total = jnp.zeros((rows, DIM), jnp.float32)
    for group in range(0, len(places), 8):
        some = places[group:group + 8]
        ids = jnp.concatenate([pay[at + ID_ROW:at + ID_ROW + 1, :CAND_ROW] for pay, at in some], axis=1)
        col = iota((rows, ids.shape[1]), 1) % CAND_ROW
        pick = (col % EXP == row[:, :1] % EXP) & (col < FB * EXP) & (ids == owner[:, :1])
        pick = jnp.where(pick, 1.0, 0.0).astype(jnp.bfloat16)
        block = jnp.concatenate([pay[at:at + CAND_ROW, :] for pay, at in some], axis=0)
        for piece in thirds(block)[::-1]:
            total += jnp.dot(pick, piece, preferred_element_type=jnp.float32)
    for ref, sums in ((keep_ref, total[:rows // 2]), (send_ref, total[rows // 2:])):
        ref[:rows // 2, :] = sums
        ref[rows // 2:rows // 2 + 8, :] = pays[0][CAND_ROW:ASK_ROW, :]
        ref[rows // 2 + 8:, :] = pays[-1][CAND_ROW:ASK_ROW, :]


def nt_dot(a, b, precision=None):
    return lax.dot_general(a, b, (((1,), (1,)), ((), ())), precision=precision, preferred_element_type=jnp.float32)


def thirds(x):
    high, low = split(x)
    return high, low, (x - high.astype(jnp.float32) - low.astype(jnp.float32)).astype(jnp.bfloat16)


def split(x):
    high = x.astype(jnp.bfloat16)
    return high, (x - high.astype(jnp.float32)).astype(jnp.bfloat16)


def at_steps(pos, steps, device, entry):
    place = jnp.zeros(entry.shape, jnp.int32)
    for i, away in enumerate(steps):
        place = jnp.where(entry // 8 == i, pos ^ away, place)
    return place == device


def largest_rows(parts, held):
    rows = []
    for top in parts:
        step = held
        while step < 8:
            top = jnp.maximum(top, pltpu.roll(top, step, 0))
            step *= 2
        rows.append(top)
    return jnp.concatenate(rows, axis=0)


def over_tokens(similar):
    return jnp.max(similar.reshape(similar.shape[0] // 8, 8, similar.shape[1]), axis=0)


def match_kernel(side, outer, asking, queries_n, held, n_tiles, n_asks, pos_ref, *refs):
    tile_refs, ask_refs = refs[:n_tiles], refs[n_tiles:n_tiles + n_asks]
    keep_ref, from_side_ref = refs[n_tiles + n_asks:n_tiles + n_asks + 2]
    *wide_refs, values_ref, chosen_ref = refs[n_tiles + n_asks + 2:]
    pos = pos_ref[0]
    n_out = 1 << len(outer)
    me_out = gather_bits(pos, outer)
    half = n_out * EXP
    tokens = jnp.concatenate([ask[...] for ask in ask_refs], axis=0)
    total = tokens.shape[0]
    lefts = []
    for ref, wide_ref in zip(tile_refs, wide_refs):
        high, low = split(ref[...])
        wide = jnp.concatenate([high, low], axis=1)
        wide_ref[...] = wide
        lefts.append((high, wide))
    parts = [[] for _ in lefts]
    for at in range(0, total, 256):
        high, low = split(tokens[at:at + 256])
        twice = jnp.concatenate([high, high], axis=1)
        for i, (left, wide) in enumerate(lefts):
            parts[i].append(over_tokens(nt_dot(wide, twice) + nt_dot(left, low)))
    largest = largest_rows([jnp.concatenate(part, axis=1) for part in parts], held)
    of_col = gather_bits(spread(iota((n_out, total), 1) // QL, steps_of(asking)), outer) ^ me_out
    member = jnp.where(of_col == iota((n_out, total), 0), 1.0 / QL, 0.0)
    values_ref[...] = nt_dot(member, largest, HIGHEST)

    cands = jnp.concatenate([keep_ref[half:, :], from_side_ref[half:, :]], axis=0)
    entries = cands.shape[0]
    own = owner_of(pos, iota((n_out, DIM), 0), outer)
    slots = chosen_ref.shape[1]
    slot = iota((entries, slots), 1)
    entry = iota((entries, slots), 0)
    same = at_steps(pos, [0, 1, side, side ^ 1], slot // CAP, entry)
    local = jnp.zeros((n_out, slots), jnp.float32)
    count = jnp.zeros((n_out, slots), jnp.float32)
    for c, at in enumerate(range(0, queries_n, DIM)):
        found = nt_dot(jnp.where(own - at == iota((n_out, DIM), 1), 1.0, 0.0), cands, HIGHEST)
        top = (CAP + 1) * c
        pick = jnp.where(same & (entry % 8 == top + slot % CAP), 1.0, 0.0)
        local += jnp.dot(found, pick, precision=HIGHEST, preferred_element_type=jnp.float32)
        pick = jnp.where(same & (entry % 8 == top + CAP), 1.0, 0.0)
        count += jnp.dot(found, pick, precision=HIGHEST, preferred_element_type=jnp.float32)
    live = (iota((n_out, slots), 1) % CAP).astype(jnp.float32) < count
    for p in range(held):
        chosen_ref[p * n_out:(p + 1) * n_out, :] = jnp.where(live & (local == float(p)), 1.0, 0.0)


def score_kernel(side, outer, held, n_tiles, pos_ref, *refs):
    wide_refs = refs[:n_tiles]
    values_ref, chosen_ref, mine_ref, theirs_ref, out_ref = refs[n_tiles:]
    pos = pos_ref[0]
    n_out = 1 << len(outer)
    half = n_out * EXP
    sums = mine_ref[...] + theirs_ref[...]
    scale = lax.rsqrt(jnp.mean(sums * sums, axis=1, keepdims=True) + 1e-05)
    order = (iota((half, 1), 0) % EXP).astype(jnp.float32)
    extra = sums * (scale * (BETA * jnp.log((NCENT + 1.0) / (order + 1.0))))
    if half % DIM > 0:
        extra = jnp.concatenate([extra, jnp.zeros((-half % DIM, DIM), jnp.float32)], axis=0)
    parts = [[] for _ in wide_refs]
    for at in range(0, half, DIM):
        high, low = split(extra[at:at + DIM])
        right = jnp.concatenate([
            jnp.concatenate([high, high], axis=1),
            jnp.concatenate([low, jnp.zeros_like(low)], axis=1),
        ], axis=0)
        for i, wide in enumerate(wide_refs):
            both = nt_dot(wide[...], right)
            parts[i].append(over_tokens(both[:, :DIM] + both[:, DIM:]))
    largest = largest_rows([jnp.concatenate(part, axis=1) for part in parts], held)
    total = largest.shape[1]
    col = iota((n_out, 3 * total), 1) % total
    member = jnp.where(col // EXP == iota((n_out, 3 * total), 0), 1.0 / QL, 0.0).astype(jnp.bfloat16)
    values = values_ref[...] + nt_dot(member, jnp.concatenate(thirds(largest), axis=1))
    slots = out_ref.shape[1]
    padded = slots + (-slots % DIM)
    shape = (n_tiles * 8, held * padded)
    entry = iota(shape, 0)
    col = iota(shape, 1)
    same = at_steps(pos, [0, side, 1, side ^ 1], col % padded // CAP, entry) & (col % padded < slots)
    pick = jnp.where(same & (entry % 8 == col // padded), 1.0, 0.0).astype(jnp.bfloat16)
    found = jnp.dot(jnp.concatenate(thirds(values), axis=0), pick, preferred_element_type=jnp.float32)
    found = found[:n_out] + found[n_out:2 * n_out] + found[2 * n_out:]
    result = jnp.zeros((n_out, slots), jnp.float32)
    for p in range(held):
        value = found[:, p * padded:p * padded + slots]
        result = jnp.where(chosen_ref[p * n_out:(p + 1) * n_out, :] > 0.5, value, result)
    out_ref[...] = result


def call(kernel, outs, *args, copied=False):
    smem = pl.BlockSpec(memory_space=pltpu.SMEM)
    vmem = pl.BlockSpec(memory_space=pltpu.VMEM)
    specs = [smem if a.ndim == 1 else vmem for a in args]
    scratch = []
    if copied:
        specs[1:] = [pl.BlockSpec(memory_space=pltpu.HBM)] * (len(args) - 1)
        scratch = [(pltpu.SMEM if a.ndim == 1 else pltpu.VMEM)(a.shape, a.dtype) for a in args[1:]]
        scratch += [pltpu.SemaphoreType.DMA((len(args) - 1,))]
        args = args[:1] + tuple(pltpu.with_memory_space_constraint(a, pltpu.HBM) for a in args[1:])
    return pl.pallas_call(
        kernel,
        out_shape=[pltpu.VMEM(o.shape, o.dtype) for o in outs] if len(outs) > 1 else outs[0],
        in_specs=specs,
        out_specs=[vmem] * len(outs) if len(outs) > 1 else vmem,
        scratch_shapes=scratch,
        compiler_params=pltpu.CompilerParams(vmem_limit_bytes=24 * 1024 * 1024),
    )(*args)


def body(queries, passages, clusters, lengths, feedback, ranks, cand_local, cand_count):
    held, tokens, _ = passages.shape
    queries_n = feedback.shape[0]
    n_corpus = lax.axis_size("corpus")
    devices = lax.axis_size("query") * n_corpus
    side, last = n_corpus | 1, 2 * n_corpus
    masks = [1 << k for k in range(devices.bit_length() - 1)]
    outer = [m for m in masks if m >= last] + [m for m in reversed(masks) if 1 < m < n_corpus]
    asking = outer[-1:] + outer[:-1]
    n_out = 1 << len(outer)
    pos = lax.axis_index(AXES).astype(jnp.int32).reshape(1)

    def swap(x, mask):
        return lax.ppermute(x, AXES, [(i, i ^ mask) for i in range(devices)])

    def struct(rows, cols=DIM):
        return jax.ShapeDtypeStruct((rows, cols), jnp.float32)

    chunks = -(-queries_n // DIM)
    pay_rows = ASK_ROW
    assert (CAP + 1) * chunks <= 8 and queries.shape[0] == 1 and 8 % held == 0
    tiles = jnp.transpose(passages, (1, 0, 2)).reshape(tokens * held, DIM)
    masked, pay = call(
        functools.partial(pairs_kernel, queries_n, held, tokens),
        [struct(tokens * held), struct(pay_rows)],
        pos, lengths, tiles, clusters, feedback.T, ranks.T, cand_local.T, cand_count.T, copied=True,
    )
    def together(*xs):
        return lax.optimization_barrier(xs)

    def joined(xs):
        return xs[0] if len(xs) == 1 else jnp.concatenate(xs, axis=0)

    beside = swap(pay, 1)
    half = n_out * EXP
    keep, send = call(functools.partial(combine_kernel, side, outer), [struct(half + 16)] * 2, pos, pay, beside)
    from_side = swap(send, side)
    sums = keep[:half] + from_side[:half]
    asks = [queries[0]]
    for step in steps_of(asking):
        asks = asks + [swap(joined(asks), step)]
    masked, _ = lax.optimization_barrier((masked, asks[1]))
    far = swap(masked, side)
    steps = steps_of(outer)
    for step in steps[:-1]:
        sums = sums + swap(sums, step)
    far, sums, asks = lax.optimization_barrier((far, sums, asks))
    came = swap(sums, steps[-1])
    tiles = [masked, far]
    tiles = tiles + [swap(t, 1) for t in tiles]
    slots = devices * CAP
    wide = jax.ShapeDtypeStruct((tokens * held, 2 * DIM), jnp.bfloat16)
    *tiles, values, chosen = call(
        functools.partial(match_kernel, side, outer, asking, queries_n, held, len(tiles), len(asks)),
        [wide] * len(tiles) + [struct(n_out, 8 * len(tiles)), struct(held * n_out, slots)],
        pos, *tiles, *asks, keep, from_side,
    )
    table = call(
        functools.partial(score_kernel, side, outer, held, len(tiles)), [struct(n_out, slots)],
        pos, *tiles, values, chosen, sums, came,
    )
    for step in reversed(steps):
        table = table + swap(table, step)
    return lax.dynamic_slice(table, (gather_bits(pos[0], outer), 0), (1, slots))


def solution(mesh):
    in_specs = (
        P(AXES, None, None),
        P(AXES, None, None),
        P(AXES, None),
        P(AXES),
        P(),
        P(),
        P(None, AXES),
        P(None, AXES),
    )
    return jax.shard_map(body, mesh=mesh, in_specs=in_specs, out_specs=P(AXES, None), check_vma=False)
```

```python
import functools

import jax
import jax.numpy as jnp
from jax import lax
from jax.experimental import pallas as pl
from jax.experimental.pallas import tpu as pltpu
from jax.sharding import PartitionSpec as P

DIM = 128
QL = 32
NCENT = 24
EXP = 10
CAP = 2
FB = 3
BETA = 0.5
AXES = ("query", "corpus")
ID_ROW = 31
CAND_ROW = 32
ASK_ROW = 40
HIGHEST = lax.Precision.HIGHEST


def iota(shape, axis):
    return lax.broadcasted_iota(jnp.int32, shape, axis)


def spread(index, steps):
    total = 0
    for k, step in enumerate(steps):
        total = total ^ (((index >> k) & 1) * step)
    return total


def gather_bits(device, bits):
    total = 0
    for k, bit in enumerate(bits):
        total = total | (jnp.where((device & bit) != 0, 1, 0) << k)
    return total


def steps_of(bits):
    return [bit | 1 for bit in bits]


def owner_of(pos, index, bits):
    return pos ^ spread(gather_bits(pos, bits) ^ index, steps_of(bits))


def pairs_kernel(queries_n, held, tokens, pos_ref, *refs):
    sources, (masked_ref, pay_ref) = refs[:7], refs[7:9]
    landed, sems = refs[9:16], refs[16]
    copies = [pltpu.make_async_copy(a, b, sems.at[k]) for k, (a, b) in enumerate(zip(sources, landed))]
    for copy in copies[::-1]:
        copy.start()
    for copy in copies[:1] + copies[2:]:
        copy.wait()
    len_ref, tiles_ref, clusters_ref, feedback_ref, ranks_ref, local_ref, count_ref = landed
    pos = pos_ref[0]
    nearby = feedback_ref[...] - pos * held
    number = (iota(nearby.shape, 0) * queries_n + iota(nearby.shape, 1)) * held + nearby
    here = (nearby >= 0) & (nearby < held)
    key = jnp.where(here, number, 0).astype(jnp.float32)
    least = jnp.min(jnp.where(here, key, 1e9))
    most = jnp.max(key)
    keys = [least, jnp.sum(key) - least - most, most]
    ranks = ranks_ref[...].astype(jnp.float32)
    lane = iota(ranks.shape, 1)
    pay_ref[:ASK_ROW, :] = jnp.zeros((ASK_ROW, DIM), jnp.float32)
    ids = jnp.zeros((1, DIM), jnp.float32)
    slot = iota((1, DIM), 1) // EXP
    kinds = iota((NCENT, tokens), 0)
    times = iota((EXP, tokens), 1)
    wanted = iota((EXP, tokens), 0).astype(jnp.float32)
    pairs = []
    for s in range(FB):
        whole = keys[s].astype(jnp.int32)
        p = whole % held
        q = (whole // held) % queries_n
        ids = jnp.where(slot == s, q.astype(jnp.float32), ids)
        rank = jnp.sum(jnp.where(lane == q, ranks, 0.0), axis=1, keepdims=True)
        kind = clusters_ref[pl.ds(p, 1), :]
        of_token = jnp.sum(jnp.where(kind == kinds, rank, 0.0), axis=0, keepdims=True)
        pairs.append((p, jnp.where((of_token == wanted) & (times < len_ref[p]), 1.0, 0.0).astype(jnp.bfloat16)))
    copies[1].wait()
    for s, (p, chosen) in enumerate(pairs):
        passage = tiles_ref[pl.ds(p, tokens, stride=held), :]
        pieces = jnp.dot(chosen, jnp.concatenate(thirds(passage), axis=1), preferred_element_type=jnp.float32)
        pay_ref[s * EXP:(s + 1) * EXP, :] = pieces[:, 2 * DIM:] + pieces[:, DIM:2 * DIM] + pieces[:, :DIM]
    per_tile = 8 // held
    row = iota((8, DIM), 0)
    limit = jnp.zeros((8, DIM), jnp.int32)
    for p in range(held):
        limit = jnp.where(row % held == p, len_ref[p], limit)
    first = tiles_ref[0:held, :]
    first = jnp.concatenate([first] * per_tile, axis=0)
    groups = tokens * held // 8
    token = iota((groups, 8, DIM), 0) * per_tile + (iota((groups, 8, DIM), 1) // held)
    tiles = tiles_ref[...].reshape(groups, 8, DIM)
    masked_ref[...] = jnp.where(token < limit[None], tiles, first[None]).reshape(groups * 8, DIM)

    pay_ref[ID_ROW:ID_ROW + 1, :] = ids
    for c, at in enumerate(range(0, queries_n, DIM)):
        width = min(DIM, queries_n - at)
        top = CAND_ROW + (CAP + 1) * c
        pay_ref[top:top + CAP, 0:width] = local_ref[:, at:at + width].astype(jnp.float32)
        pay_ref[top + CAP:top + CAP + 1, 0:width] = count_ref[:, at:at + width].astype(jnp.float32)


def combine_kernel(side, outer, pos_ref, *refs):
    *pays, keep_ref, send_ref = refs
    pos = pos_ref[0]
    half = (1 << len(outer)) * EXP
    rows = 2 * half
    row = iota((rows, DIM), 0)
    owner = owner_of(pos, row % half // EXP, outer) ^ ((row // half) * side)
    owner = owner.astype(jnp.float32)
    places = [(pay, 0) for pay in pays]
    total = jnp.zeros((rows, DIM), jnp.float32)
    for group in range(0, len(places), 8):
        some = places[group:group + 8]
        ids = jnp.concatenate([pay[at + ID_ROW:at + ID_ROW + 1, :CAND_ROW] for pay, at in some], axis=1)
        col = iota((rows, ids.shape[1]), 1) % CAND_ROW
        pick = (col % EXP == row[:, :1] % EXP) & (col < FB * EXP) & (ids == owner[:, :1])
        pick = jnp.where(pick, 1.0, 0.0).astype(jnp.bfloat16)
        block = jnp.concatenate([pay[at:at + CAND_ROW, :] for pay, at in some], axis=0)
        for piece in thirds(block)[::-1]:
            total += jnp.dot(pick, piece, preferred_element_type=jnp.float32)
    for ref, sums in ((keep_ref, total[:rows // 2]), (send_ref, total[rows // 2:])):
        ref[:rows // 2, :] = sums
        ref[rows // 2:rows // 2 + 8, :] = pays[0][CAND_ROW:ASK_ROW, :]
        ref[rows // 2 + 8:, :] = pays[-1][CAND_ROW:ASK_ROW, :]


def nt_dot(a, b, precision=None):
    return lax.dot_general(a, b, (((1,), (1,)), ((), ())), precision=precision, preferred_element_type=jnp.float32)


def thirds(x):
    high, low = split(x)
    return high, low, (x - high.astype(jnp.float32) - low.astype(jnp.float32)).astype(jnp.bfloat16)


def split(x):
    high = x.astype(jnp.bfloat16)
    return high, (x - high.astype(jnp.float32)).astype(jnp.bfloat16)


def at_steps(pos, steps, device, entry):
    place = jnp.zeros(entry.shape, jnp.int32)
    for i, away in enumerate(steps):
        place = jnp.where(entry // 8 == i, pos ^ away, place)
    return place == device


def largest_rows(parts, held):
    rows = []
    for top in parts:
        step = held
        while step < 8:
            top = jnp.maximum(top, pltpu.roll(top, step, 0))
            step *= 2
        rows.append(top)
    return jnp.concatenate(rows, axis=0)


def over_tokens(similar):
    return jnp.max(similar.reshape(similar.shape[0] // 8, 8, similar.shape[1]), axis=0)


def match_kernel(side, outer, asking, queries_n, held, n_tiles, n_asks, pos_ref, *refs):
    tile_refs, ask_refs = refs[:n_tiles], refs[n_tiles:n_tiles + n_asks]
    keep_ref, from_side_ref = refs[n_tiles + n_asks:n_tiles + n_asks + 2]
    *wide_refs, values_ref, chosen_ref = refs[n_tiles + n_asks + 2:]
    pos = pos_ref[0]
    n_out = 1 << len(outer)
    me_out = gather_bits(pos, outer)
    half = n_out * EXP
    tokens = jnp.concatenate([ask[...] for ask in ask_refs], axis=0)
    total = tokens.shape[0]
    lefts = []
    for ref, wide_ref in zip(tile_refs, wide_refs):
        high, low = split(ref[...])
        wide = jnp.concatenate([high, low], axis=1)
        wide_ref[...] = wide
        lefts.append((high, wide))
    parts = [[] for _ in lefts]
    for at in range(0, total, 256):
        high, low = split(tokens[at:at + 256])
        twice = jnp.concatenate([high, high], axis=1)
        for i, (left, wide) in enumerate(lefts):
            parts[i].append(over_tokens(nt_dot(wide, twice) + nt_dot(left, low)))
    largest = largest_rows([jnp.concatenate(part, axis=1) for part in parts], held)
    of_col = gather_bits(spread(iota((n_out, total), 1) // QL, steps_of(asking)), outer) ^ me_out
    member = jnp.where(of_col == iota((n_out, total), 0), 1.0 / QL, 0.0)
    values_ref[...] = nt_dot(member, largest, HIGHEST)

    cands = jnp.concatenate([keep_ref[half:, :], from_side_ref[half:, :]], axis=0)
    entries = cands.shape[0]
    own = owner_of(pos, iota((n_out, DIM), 0), outer)
    slots = chosen_ref.shape[1]
    slot = iota((entries, slots), 1)
    entry = iota((entries, slots), 0)
    same = at_steps(pos, [0, 1, side, side ^ 1], slot // CAP, entry)
    local = jnp.zeros((n_out, slots), jnp.float32)
    count = jnp.zeros((n_out, slots), jnp.float32)
    for c, at in enumerate(range(0, queries_n, DIM)):
        found = nt_dot(jnp.where(own - at == iota((n_out, DIM), 1), 1.0, 0.0), cands, HIGHEST)
        top = (CAP + 1) * c
        pick = jnp.where(same & (entry % 8 == top + slot % CAP), 1.0, 0.0)
        local += jnp.dot(found, pick, precision=HIGHEST, preferred_element_type=jnp.float32)
        pick = jnp.where(same & (entry % 8 == top + CAP), 1.0, 0.0)
        count += jnp.dot(found, pick, precision=HIGHEST, preferred_element_type=jnp.float32)
    live = (iota((n_out, slots), 1) % CAP).astype(jnp.float32) < count
    for p in range(held):
        chosen_ref[p * n_out:(p + 1) * n_out, :] = jnp.where(live & (local == float(p)), 1.0, 0.0)


def score_kernel(side, outer, held, n_tiles, own, pos_ref, *refs):
    wide_refs = refs[:n_tiles]
    values_ref, chosen_ref, mine_ref, theirs_ref, out_ref = refs[n_tiles:]
    pos = pos_ref[0]
    n_out = 1 << (len(outer) - 1)
    half = n_out * EXP
    upper = ((pos & outer[-1]) != 0) == own

    def of_half(low, high):
        return jnp.where(upper, high, low)

    sums = of_half(mine_ref[:half, :], mine_ref[half:, :]) + of_half(theirs_ref[:half, :], theirs_ref[half:, :])
    scale = lax.rsqrt(jnp.mean(sums * sums, axis=1, keepdims=True) + 1e-05)
    order = (iota((half, 1), 0) % EXP).astype(jnp.float32)
    extra = sums * (scale * (BETA * jnp.log((NCENT + 1.0) / (order + 1.0))))
    if half % DIM > 0:
        extra = jnp.concatenate([extra, jnp.zeros((-half % DIM, DIM), jnp.float32)], axis=0)
    parts = [[] for _ in wide_refs]
    for at in range(0, half, DIM):
        high, low = split(extra[at:at + DIM])
        right = jnp.concatenate([
            jnp.concatenate([high, high], axis=1),
            jnp.concatenate([low, jnp.zeros_like(low)], axis=1),
        ], axis=0)
        for i, wide in enumerate(wide_refs):
            both = nt_dot(wide[...], right)
            parts[i].append(over_tokens(both[:, :DIM] + both[:, DIM:]))
    largest = largest_rows([jnp.concatenate(part, axis=1) for part in parts], held)
    total = largest.shape[1]
    col = iota((n_out, 3 * total), 1) % total
    member = jnp.where(col // EXP == iota((n_out, 3 * total), 0), 1.0 / QL, 0.0).astype(jnp.bfloat16)
    values = of_half(values_ref[:n_out, :], values_ref[n_out:, :]) + nt_dot(member, jnp.concatenate(thirds(largest), axis=1))
    slots = out_ref.shape[1]
    padded = slots + (-slots % DIM)
    shape = (n_tiles * 8, held * padded)
    entry = iota(shape, 0)
    col = iota(shape, 1)
    same = at_steps(pos, [0, side, 1, side ^ 1], col % padded // CAP, entry) & (col % padded < slots)
    pick = jnp.where(same & (entry % 8 == col // padded), 1.0, 0.0).astype(jnp.bfloat16)
    found = jnp.dot(jnp.concatenate([t.astype(jnp.float32) for t in thirds(values)], axis=0).astype(jnp.bfloat16), pick, preferred_element_type=jnp.float32)
    found = found[:n_out] + found[n_out:2 * n_out] + found[2 * n_out:]
    result = jnp.zeros((n_out, slots), jnp.float32)
    for p in range(held):
        value = found[:, p * padded:p * padded + slots]
        at = 2 * p * n_out
        chosen = of_half(chosen_ref[at:at + n_out, :], chosen_ref[at + n_out:at + 2 * n_out, :])
        result = jnp.where(chosen > 0.5, value, result)
    out_ref[...] = result


def call(kernel, outs, *args, copied=False):
    smem = pl.BlockSpec(memory_space=pltpu.SMEM)
    vmem = pl.BlockSpec(memory_space=pltpu.VMEM)
    specs = [smem if a.ndim == 1 else vmem for a in args]
    scratch = []
    if copied:
        specs[1:] = [pl.BlockSpec(memory_space=pltpu.HBM)] * (len(args) - 1)
        scratch = [(pltpu.SMEM if a.ndim == 1 else pltpu.VMEM)(a.shape, a.dtype) for a in args[1:]]
        scratch += [pltpu.SemaphoreType.DMA((len(args) - 1,))]
        args = args[:1] + tuple(pltpu.with_memory_space_constraint(a, pltpu.HBM) for a in args[1:])
    return pl.pallas_call(
        kernel,
        out_shape=[pltpu.VMEM(o.shape, o.dtype) for o in outs] if len(outs) > 1 else outs[0],
        in_specs=specs,
        out_specs=[vmem] * len(outs) if len(outs) > 1 else vmem,
        scratch_shapes=scratch,
        compiler_params=pltpu.CompilerParams(vmem_limit_bytes=24 * 1024 * 1024),
    )(*args)


def body(queries, passages, clusters, lengths, feedback, ranks, cand_local, cand_count):
    held, tokens, _ = passages.shape
    queries_n = feedback.shape[0]
    n_corpus = lax.axis_size("corpus")
    devices = lax.axis_size("query") * n_corpus
    side, last = n_corpus | 1, 2 * n_corpus
    masks = [1 << k for k in range(devices.bit_length() - 1)]
    outer = [m for m in masks if m >= last] + [m for m in reversed(masks) if 1 < m < n_corpus]
    asking = outer[-1:] + outer[:-1]
    n_out = 1 << len(outer)
    pos = lax.axis_index(AXES).astype(jnp.int32).reshape(1)

    def swap(x, mask):
        return lax.ppermute(x, AXES, [(i, i ^ mask) for i in range(devices)])

    def struct(rows, cols=DIM):
        return jax.ShapeDtypeStruct((rows, cols), jnp.float32)

    chunks = -(-queries_n // DIM)
    pay_rows = ASK_ROW
    assert (CAP + 1) * chunks <= 8 and queries.shape[0] == 1 and 8 % held == 0
    tiles = jnp.transpose(passages, (1, 0, 2)).reshape(tokens * held, DIM)
    masked, pay = call(
        functools.partial(pairs_kernel, queries_n, held, tokens),
        [struct(tokens * held), struct(pay_rows)],
        pos, lengths, tiles, clusters, feedback.T, ranks.T, cand_local.T, cand_count.T, copied=True,
    )
    def together(*xs):
        return lax.optimization_barrier(xs)

    def joined(xs):
        return xs[0] if len(xs) == 1 else jnp.concatenate(xs, axis=0)

    beside = swap(pay, 1)
    half = n_out * EXP
    keep, send = call(functools.partial(combine_kernel, side, outer), [struct(half + 16)] * 2, pos, pay, beside)
    from_side = swap(send, side)
    sums = keep[:half] + from_side[:half]
    asks = [queries[0]]
    for step in steps_of(asking):
        asks = asks + [swap(joined(asks), step)]
    masked, _ = lax.optimization_barrier((masked, asks[1]))
    far = swap(masked, side)
    steps = steps_of(outer)
    for step in steps[:-1]:
        sums = sums + swap(sums, step)
    far, sums, asks = lax.optimization_barrier((far, sums, asks))
    came = swap(sums, steps[-1])
    tiles = [masked, far]
    tiles = tiles + [swap(t, 1) for t in tiles]
    slots = devices * CAP
    wide = jax.ShapeDtypeStruct((tokens * held, 2 * DIM), jnp.bfloat16)
    *tiles, values, chosen = call(
        functools.partial(match_kernel, side, outer, asking, queries_n, held, len(tiles), len(asks)),
        [wide] * len(tiles) + [struct(n_out, 8 * len(tiles)), struct(held * n_out, slots)],
        pos, *tiles, *asks, keep, from_side,
    )
    theirs, mine = [
        call(
            functools.partial(score_kernel, side, outer, held, len(tiles), own), [struct(n_out // 2, slots)],
            pos, *tiles, values, chosen, sums, came,
        ) for own in (False, True)
    ]
    table = mine + swap(theirs, steps[-1])
    for step in reversed(steps[:-1]):
        table = table + swap(table, step)
    return lax.dynamic_slice(table, (gather_bits(pos[0], outer[:-1]), 0), (1, slots))


def solution(mesh):
    in_specs = (
        P(AXES, None, None),
        P(AXES, None, None),
        P(AXES, None),
        P(AXES),
        P(),
        P(),
        P(None, AXES),
        P(None, AXES),
    )
    return jax.shard_map(body, mesh=mesh, in_specs=in_specs, out_specs=P(AXES, None), check_vma=False)
```
